32 devices in a mesh: grp: 4 (over z), dev: 8 (over y, x, core).
Axes of the slice: x: 2, y: 2, z: 4, core: 2. Of those that a mesh axis runs over, the one named last changes fastest.
Arguments:
- tracer: float32 [72, 16, 4096], P(None, None, ('grp', 'dev')), may hold values from -6 to 6
- metric: float32 [4096], P(('grp', 'dev')), may hold values from 0.5 to 2
- coef: float32 [72, 65536], P(None, ('grp', 'dev')), may hold values from 0.02 to 601
- nbr_slot: int32 [4, 4096], P(None, ('grp', 'dev')), may hold values from 0 to 559, as said below
- edge_flip: int32 [4, 4096], P(None, ('grp', 'dev')), may hold values from 0 to 1, as said below
- send_slot: int32 [1536], P(('grp', 'dev')), may hold values from 0 to 511, as said below
- span_slot: int32 [16, 4096], P(None, ('grp', 'dev')), may hold values from 0 to 16383, as said below
Outputs:
- mixed: float32 [72, 16, 4096], P(None, None, ('grp', 'dev'))
The draws below stay inside these ranges and needn't reach their ends.
Inputs may be any that keep to these rules, and one draw needn't show every extreme that they name: `nbr_slot`: entries below 512 name an edge of an element of the same device as s * 128 + e; larger ones name the neighbouring devices' buffer entries in the order of the edge table. Each element edge meets exactly one other edge, both ways. `edge_flip`: symmetric over the two sides of a shared edge. `send_slot`: each entry is an own edge s * 128 + e'. For each device, 16 own edges whose neighbours lie on device (g + 1, v), 16 for (g - 1, v), 8 for (g, v + 1), 8 for (g, v - 1), in the order the receiving edge table expects. `span_slot`: within each group along dev the values form a permutation of 0 to 16383, and every device holds exactly 256 columns whose value lies in each range r * 2048 to (r + 1) * 2048 - 1.
All inputs are finite; a program needn't handle non-finite values.
Results may differ from the reference program's by a relative error of at most 0.0003.
Values sent between devices are 32-bit elements; how exact they have to be, the bound alone decides.
A program may use at most 64 MiB of HBM per device.

```python
import math
import jax
import jax.numpy as jnp
import numpy as np
from jax import lax

LEV = 72
BR = 8
BC = 16
E_DEV = 128
COLS_DEV = 2048
ELEMS = 4096
COLUMNS = 65536
N_GRP = 4
N_DEV = 8


def block_geometry(key):
    devices = N_GRP * N_DEV
    rotation = jax.random.randint(jax.random.fold_in(key, 11), (N_GRP * BR, N_DEV * BC), 0, 4).astype(jnp.int32)
    dev_keys = jax.random.split(jax.random.fold_in(key, 12), devices)
    slot_pos = jax.vmap(lambda one_key: jax.random.permutation(one_key, E_DEV))(dev_keys).astype(jnp.int32)
    pos_slot = jnp.argsort(slot_pos, axis=1).astype(jnp.int32)
    dev_ids = jnp.arange(devices, dtype=jnp.int32)[:, None]
    return (rotation, slot_pos, pos_slot, dev_ids // N_DEV, dev_ids % N_DEV)


def neighbour_tables(key):
    rotation, slot_pos, pos_slot, grp_idx, dev_idx = block_geometry(key)
    grid_row = grp_idx * BR + slot_pos // BC
    grid_col = dev_idx * BC + slot_pos % BC
    turns = rotation[grid_row, grid_col]
    local_side = jnp.arange(4, dtype=jnp.int32)[:, None, None]
    facing = (local_side + turns[None]) % 4
    step_row = jnp.array([-1, 0, 1, 0], jnp.int32)[facing]
    step_col = jnp.array([0, 1, 0, -1], jnp.int32)[facing]
    next_row = (grid_row[None] + step_row) % (N_GRP * BR)
    next_col = (grid_col[None] + step_col) % (N_DEV * BC)
    next_dev = next_row // BR * N_DEV + next_col // BC
    in_row = next_row % BR
    in_col = next_col % BC
    next_slot = pos_slot[next_dev, in_row * BC + in_col]
    next_turns = rotation[next_row, next_col]
    next_side = (facing + 2 - next_turns) % 4
    home_dev = (grp_idx * N_DEV + dev_idx)[None]
    own_count = 4 * E_DEV
    remote = jnp.where(facing == 0, own_count + in_col, jnp.where(facing == 2, own_count + BC + in_col, jnp.where(facing == 3, own_count + 2 * BC + in_row, own_count + 2 * BC + BR + in_row)))
    slot_index = jnp.where(next_dev == home_dev, next_side * E_DEV + next_slot, remote)
    tangent_sign = jnp.array([[1, 1, -1, -1], [1, -1, -1, 1]], jnp.int32)
    flip_bits = (tangent_sign[local_side % 2, turns[None]] != tangent_sign[next_side % 2, next_turns]).astype(jnp.int32)
    return (slot_index.reshape(4, -1).astype(jnp.int32), flip_bits.reshape(4, -1))


def draw_nbr_slot(key, part):
    return neighbour_tables(key)[0]


def draw_edge_flip(key, part):
    return neighbour_tables(key)[1]


def draw_send_slot(key, part):
    rotation, slot_pos, pos_slot, grp_idx, dev_idx = block_geometry(key)

    def outward(rows_at, cols_at, facing):
        slot_here = pos_slot[:, rows_at * BC + cols_at]
        turns = rotation[grp_idx * BR + rows_at[None], dev_idx * BC + cols_at[None]]
        return (facing - turns) % 4 * E_DEV + slot_here
    along_cols = jnp.arange(BC, dtype=jnp.int32)
    along_rows = jnp.arange(BR, dtype=jnp.int32)
    pieces = [outward(BR - 1 + 0 * along_cols, along_cols, 2), outward(0 * along_cols, along_cols, 0), outward(along_rows, BC - 1 + 0 * along_rows, 1), outward(along_rows, 0 * along_rows, 3)]
    return jnp.concatenate(pieces, axis=1).reshape(-1).astype(jnp.int32)


def draw_span_slot(key, part):
    devices = N_GRP * N_DEV
    per_peer = COLS_DEV // N_DEV
    rank_keys = jax.random.split(jax.random.fold_in(key, 21), devices)
    place_keys = jax.random.split(jax.random.fold_in(key, 22), devices)
    ranks = jax.vmap(lambda one_key: jax.random.permutation(one_key, COLS_DEV))(rank_keys).astype(jnp.int32)
    arrivals = jax.vmap(lambda one_key: jax.random.permutation(one_key, COLS_DEV))(place_keys).astype(jnp.int32)
    dev_ids = jnp.arange(devices, dtype=jnp.int32)
    target = ranks // per_peer
    within = ranks % per_peer
    arrival_idx = (dev_ids % N_DEV)[:, None] * per_peer + within
    target_dev = (dev_ids // N_DEV)[:, None] * N_DEV + target
    position = arrivals[target_dev, arrival_idx]
    slot_value = target * COLS_DEV + position
    return slot_value.reshape(devices, 16, E_DEV).transpose(1, 0, 2).reshape(16, devices * E_DEV).astype(jnp.int32)


def draw_coef(key, part):
    column_key = jax.random.fold_in(key, 31)
    level_key = jax.random.fold_in(key, 32)
    level_factor = jnp.exp(jax.random.uniform(level_key, (LEV, COLUMNS), jnp.float32, -math.log(2.0), math.log(2.0)))
    column_scale = jnp.exp(jax.random.uniform(column_key, (COLUMNS,), jnp.float32, math.log(0.05), math.log(300.0)))
    return (column_scale[None, :] * level_factor).astype(jnp.float32)


def block_scale(stream_key, dims, cuts, smallest, high):
    def one(dim, parts):
        steps = jax.random.uniform(jax.random.fold_in(jax.random.fold_in(stream_key, 6), dim), (parts,), jnp.float32, smallest / len(cuts), high / len(cuts))
        return jnp.repeat(jnp.exp(steps), dims[dim] // parts).reshape((-1,) + (1,) * (len(dims) - dim - 1))

    loudness = one(*cuts[0])
    for cut in cuts[1:]:
        loudness = loudness * one(*cut)
    return loudness


def normal_values(stream_key, dims, scale, most, cuts=(), kind=jnp.bfloat16):
    factor_of = block_scale(stream_key, dims, cuts, -0.22, 0.18) if cuts else 1.0
    result = jax.random.normal(stream_key, dims, jnp.float32) * scale * factor_of
    return jnp.minimum(jnp.maximum(result, -most), most).astype(kind)


def setup_inputs(seed: int = 0) -> dict:
    key_list = jax.random.split(jax.random.key(seed), 8)
    return {
        "tracer": normal_values(key_list[0], (LEV, 16, ELEMS), 1.0, 6.0, ((2, 32),), jnp.float32),
        "metric": jnp.clip(jnp.exp(math.log(2.0) - 1.3862944 * jax.random.uniform(key_list[1], (ELEMS,), jnp.float32) ** block_scale(key_list[1], (ELEMS,), ((0, 32),), -0.2, 0.2)), 0.5, 2.0),
        "coef": draw_coef(jax.random.fold_in(key_list[7], 71), 0),
        "nbr_slot": draw_nbr_slot(jax.random.fold_in(key_list[7], 71), 0),
        "edge_flip": draw_edge_flip(jax.random.fold_in(key_list[7], 71), 0),
        "send_slot": draw_send_slot(jax.random.fold_in(key_list[7], 71), 0),
        "span_slot": draw_span_slot(jax.random.fold_in(key_list[7], 71), 0),
    }


PENALTY = 10.0
HYPER = 0.0001

def gll_tables():
    gll_nodes = np.array([-1.0, -1.0 / np.sqrt(5.0), 1.0 / np.sqrt(5.0), 1.0])
    weights = np.array([1.0 / 6.0, 5.0 / 6.0, 5.0 / 6.0, 1.0 / 6.0])
    lambdas = np.ones(4)
    for jdx in range(4):
        for kdx in range(4):
            if kdx != jdx:
                lambdas[jdx] = lambdas[jdx] / (gll_nodes[jdx] - gll_nodes[kdx])
    derivative = np.zeros((4, 4))
    for idx in range(4):
        for jdx in range(4):
            if idx != jdx:
                derivative[idx, jdx] = lambdas[jdx] / lambdas[idx] / (gll_nodes[idx] - gll_nodes[jdx])
        derivative[idx, idx] = -np.sum(derivative[idx])
    stiffness = -(derivative.T * weights[None, :] @ derivative) / weights[:, None]
    identity = np.eye(4)
    lap_matrix = np.kron(stiffness, identity) + np.kron(identity, stiffness)
    edge_points = np.array([[0, 1, 2, 3], [3, 7, 11, 15], [12, 13, 14, 15], [0, 4, 8, 12]])
    edge_order = edge_points.T.reshape(-1)
    spread = np.zeros((16, 16))
    spread[edge_order, np.arange(16)] = 1.0
    return (lap_matrix.astype(np.float32), spread.astype(np.float32), edge_order.astype(np.int32))

def own_traces(block_field):
    lap_matrix, spread, edge_order = gll_tables()
    levels, points, elem_count = block_field.shape
    return jnp.take(block_field, jnp.asarray(edge_order), axis=1).reshape(levels, 4, 4 * elem_count)

def element_operator(block_field, elem_scale, neighbours, flip_bits, incoming):
    lap_matrix, spread, edge_order = gll_tables()
    levels, points, elem_count = block_field.shape
    own_edges = own_traces(block_field)
    edge_table = jnp.concatenate([own_edges, incoming], axis=2)
    across = jnp.take(edge_table, neighbours, axis=2)
    across = jnp.where(flip_bits[None, None, :] == 1, across[:, ::-1, :], across)
    jump_terms = (PENALTY * (across - own_edges)).reshape(levels, 16, elem_count)
    inner_part = jnp.einsum('pq,lqe->lpe', jnp.asarray(lap_matrix), block_field, precision=lax.Precision.HIGHEST)
    edge_part = jnp.einsum('pk,lke->lpe', jnp.asarray(spread), jump_terms, precision=lax.Precision.HIGHEST)
    return elem_scale[None, None, :] * (inner_part + edge_part)

def apply_everywhere(fields, scales, neighbours, flip_bits, send_lists):
    levels = fields.shape[1]
    width = 2 * BC + 2 * BR

    def outgoing_of(bundle):
        return jnp.take(own_traces(bundle[0]), bundle[1], axis=2)
    outgoing = lax.map(outgoing_of, (fields, send_lists)).reshape(N_GRP, N_DEV, levels, 4, width)
    from_south = jnp.roll(outgoing[..., :BC], 1, axis=0)
    from_north = jnp.roll(outgoing[..., BC:2 * BC], -1, axis=0)
    from_west = jnp.roll(outgoing[..., 2 * BC:2 * BC + BR], 1, axis=1)
    from_east = jnp.roll(outgoing[..., 2 * BC + BR:], -1, axis=1)
    incoming = jnp.concatenate([from_south, from_north, from_west, from_east], axis=-1)
    incoming = incoming.reshape(N_GRP * N_DEV, levels, 4, width)

    def operate_one(bundle):
        return element_operator(bundle[0], bundle[1], bundle[2], bundle[3], bundle[4])
    return lax.map(operate_one, (fields, scales, neighbours, flip_bits, incoming))

def vertical_solve(values, mixing):
    columns = values.shape[1]
    mixing_below = jnp.concatenate([mixing[1:], jnp.zeros((1, columns), jnp.float32)], axis=0)
    diagonal = 1.0 + mixing + mixing_below
    sub_diag = jnp.concatenate([jnp.zeros((1, columns), jnp.float32), -mixing[1:]], axis=0)
    super_diag = -mixing_below

    def forward(carry, level_in):
        upper_prev, rhs_prev = carry
        sub_here, diag_here, sup_here, rhs_here = level_in
        denom = diag_here - sub_here * upper_prev
        upper_now = sup_here / denom
        rhs_now = (rhs_here - sub_here * rhs_prev) / denom
        return ((upper_now, rhs_now), (upper_now, rhs_now))
    start = (jnp.zeros((columns,), jnp.float32), jnp.zeros((columns,), jnp.float32))
    ignored, (uppers, rhs_mod) = lax.scan(forward, start, (sub_diag, diagonal, super_diag, values))

    def backward(below, level_in):
        upper_here, rhs_here = level_in
        solved_here = rhs_here - upper_here * below
        return (solved_here, solved_here)
    ignored_too, solved = lax.scan(backward, jnp.zeros((columns,), jnp.float32), (uppers, rhs_mod), reverse=True)
    return solved

def reference(tracer, metric, coef, nbr_slot, edge_flip, send_slot, span_slot):
    devices = N_GRP * N_DEV
    fields = tracer.reshape(LEV, 16, devices, E_DEV).transpose(2, 0, 1, 3)
    scales = metric.reshape(devices, E_DEV)
    neighbours = nbr_slot.reshape(4, devices, E_DEV).transpose(1, 0, 2).reshape(devices, 4 * E_DEV)
    flip_bits = edge_flip.reshape(4, devices, E_DEV).transpose(1, 0, 2).reshape(devices, 4 * E_DEV)
    send_lists = send_slot.reshape(devices, 2 * BC + 2 * BR)
    first_pass = apply_everywhere(fields, scales, neighbours, flip_bits, send_lists)
    second = apply_everywhere(first_pass, scales, neighbours, flip_bits, send_lists)
    stepped = fields - HYPER * second
    span_ids = span_slot.reshape(16, devices, E_DEV).transpose(1, 0, 2).reshape(devices, 16 * E_DEV)
    offsets = jnp.arange(devices, dtype=jnp.int32) // N_DEV * (N_DEV * COLS_DEV)
    sources = (span_ids + offsets[:, None]).astype(jnp.int32)

    def column_step(bundle):
        mixing = jnp.take(coef, bundle[1], axis=1)
        return vertical_solve(bundle[0].reshape(LEV, COLS_DEV), mixing)
    mixed_out = lax.map(column_step, (stepped, sources))
    return mixed_out.reshape(devices, LEV, 16, E_DEV).transpose(1, 2, 0, 3).reshape(LEV, 16, devices * E_DEV)
```

```python
import functools

import jax
import jax.numpy as jnp
import numpy as np
from jax import lax
from jax.experimental import pallas as pl
from jax.experimental.pallas import tpu as pltpu
from jax.sharding import PartitionSpec as P

PENALTY = 10.0
HYPER = 0.0001
LANES = 128
MESH = pl.DeviceIdType.MESH
F32 = jnp.float32
BF16 = jnp.bfloat16
I32 = jnp.int32

EDGE_POINT = [[0, 1, 2, 3], [3, 7, 11, 15], [12, 13, 14, 15], [0, 4, 8, 12]]
EDGE_ROWS = [(0, 16, 1, 0), (16, 16, -1, 0), (32, 8, 0, 1), (40, 8, 0, -1)]


def gll_laplacian():
    gll_nodes = np.array([-1.0, -1.0 / np.sqrt(5.0), 1.0 / np.sqrt(5.0), 1.0])
    weights = np.array([1.0 / 6.0, 5.0 / 6.0, 5.0 / 6.0, 1.0 / 6.0])
    lambdas = np.ones(4)
    for jdx in range(4):
        for kdx in range(4):
            if kdx != jdx:
                lambdas[jdx] = lambdas[jdx] / (gll_nodes[jdx] - gll_nodes[kdx])
    derivative = np.zeros((4, 4))
    for idx in range(4):
        for jdx in range(4):
            if idx != jdx:
                derivative[idx, jdx] = (
                    lambdas[jdx] / lambdas[idx] / (gll_nodes[idx] - gll_nodes[jdx])
                )
        derivative[idx, idx] = -np.sum(derivative[idx])
    stiffness = -(derivative.T * weights[None, :] @ derivative) / weights[:, None]
    identity = np.eye(4)
    return np.kron(stiffness, identity) + np.kron(identity, stiffness)


def iota(shape, dim):
    return lax.broadcasted_iota(I32, shape, dim)


def one_hot(cond):
    return jnp.where(cond, 1.0, 0.0).astype(BF16)


def halves(value):
    hi = value.astype(BF16)
    lo = (value - hi.astype(F32)).astype(BF16)
    return hi, lo


def dot(a, b):
    return jnp.dot(a, b, preferred_element_type=F32)


def kernel(
    n_grp, n_dev, levels, cols,
    tr_h, met_h, coef_h, nbr_h, flip_h, send_h, span_h,
    out,
    tr_v, met_v, coef_v, nbr_v, flip_v, send_v, span_v,
    send_pos, pos_in, stack, blk_out, blk_in, spread_w,
    edge_w, send_w, edge_out, edge_in, across_v,
    field, first, col_c, lev_c, lev_b, lev_u, lev_y,
    load_sem, pos_ssem, pos_rsem, blk_ssem, blk_rsem, edge_ssem, edge_rsem,
):
    grp, dev = lax.axis_index("grp"), lax.axis_index("dev")
    points = 16
    per_peer = cols // n_dev
    width = max(per_peer, LANES)
    per_tile = width // LANES
    src_tiles = cols // LANES
    lap = gll_laplacian()

    loads = [
        pltpu.make_async_copy(src, dst, load_sem.at[i])
        for i, (src, dst) in enumerate(
            [(span_h, span_v), (tr_h, tr_v), (send_h, send_v), (coef_h, coef_v),
             (nbr_h, nbr_v), (flip_h, flip_v), (met_h, met_v)]
        )
    ]
    for load in loads:
        load.start()

    barrier = pltpu.get_barrier_semaphore()
    for d in range(1, n_dev):
        pl.semaphore_signal(
            barrier, inc=1, device_id=(grp, lax.rem(dev + d, n_dev)), device_id_type=MESH
        )
    for step in (1, n_grp - 1):
        pl.semaphore_signal(
            barrier, inc=1, device_id=(lax.rem(grp + step, n_grp), dev), device_id_type=MESH
        )

    loads[0].wait()
    span = span_v[...]
    shift = cols.bit_length() - 1
    target = span >> shift
    place = span & (cols - 1)
    hits = jnp.concatenate(
        [jnp.where(target == r, 1.0, 0.0) for r in range(n_dev)], axis=0
    ).astype(BF16)
    count = n_dev * points
    before = one_hot(iota((LANES, LANES), 0) < iota((LANES, LANES), 1))
    along = dot(hits, before)
    totals = dot(hits, jnp.ones((LANES, LANES), BF16))
    row_i, col_i = iota((count, count), 0), iota((count, count), 1)
    earlier = one_hot((col_i < row_i) & ((col_i >> 4) == (row_i >> 4)))
    ranks = along + dot(earlier, totals.astype(BF16))
    rank = jnp.zeros((points, LANES), F32)
    for r in range(n_dev):
        rank = jnp.where(target == r, ranks[r * points:(r + 1) * points], rank)
    rank = rank.astype(I32)
    sub = rank >> 7
    lane = rank & (LANES - 1)
    tile = target * per_tile + sub
    row8 = target * 8 + sub
    place_hi = (place >> 7).astype(F32)
    place_lo = (place & (LANES - 1)).astype(F32)
    rows_out = n_dev * 8
    lists = []
    for p in range(points):
        spread_w[0:LANES, p * LANES:(p + 1) * LANES] = one_hot(
            iota((LANES, LANES), 0) == lane[p:p + 1, :]
        )
        mine = iota((rows_out, LANES), 0) == row8[p:p + 1, :]
        lists.append(
            jnp.concatenate(
                [jnp.where(mine, place_hi[p:p + 1, :], 0.0), jnp.where(mine, place_lo[p:p + 1, :], 0.0)],
                axis=0,
            ).astype(BF16)
        )
    spread_w[LANES:2 * LANES, :] = spread_w[0:LANES, :]
    packed = lax.dot_general(
        jnp.concatenate(lists, axis=1),
        spread_w[0:LANES, :],
        (((1,), (1,)), ((), ())),
        preferred_element_type=F32,
    )
    send_pos[...] = packed[:rows_out] * 128.0 + packed[rows_out:]
    edge_in[0, 48:LANES, :] = jnp.zeros((LANES - 48, 3 * LANES), F32)
    edge_in[1, 48:LANES, :] = jnp.zeros((LANES - 48, 3 * LANES), F32)
    send_w[...] = jnp.zeros(send_w.shape, BF16)

    pl.semaphore_wait(barrier, n_dev + 1)

    def pos_copy(peer, slot):
        return pltpu.make_async_remote_copy(
            src_ref=send_pos.at[pl.ds(pl.multiple_of(peer * 8, 8), 8), :],
            dst_ref=pos_in.at[slot],
            send_sem=pos_ssem.at[peer],
            recv_sem=pos_rsem.at[slot],
            device_id=(grp, peer),
            device_id_type=MESH,
        )

    def blk_copy(peer, slot):
        return pltpu.make_async_remote_copy(
            src_ref=blk_out.at[peer],
            dst_ref=blk_in.at[slot],
            send_sem=blk_ssem.at[peer],
            recv_sem=blk_rsem.at[slot],
            device_id=(grp, peer),
            device_id_type=MESH,
        )

    def edge_copies(turn):
        return [
            pltpu.make_async_remote_copy(
                src_ref=edge_out.at[turn, pl.ds(at, rows), :],
                dst_ref=edge_in.at[turn, pl.ds(at, rows), :],
                send_sem=edge_ssem.at[turn, k],
                recv_sem=edge_rsem.at[turn, k],
                device_id=(lax.rem(grp + n_grp + dg, n_grp), lax.rem(dev + n_dev + dv, n_dev)),
                device_id_type=MESH,
            )
            for k, (at, rows, dg, dv) in enumerate(EDGE_ROWS)
        ]

    def start_pos(d, carry):
        pos_copy(lax.rem(dev + d, n_dev), dev).start()
        return carry

    lax.fori_loop(1, n_dev, start_pos, 0)

    for load in loads[1:]:
        load.wait()
    send_w[:, 0:48] = one_hot(iota((4 * LANES, 48), 0) == send_v[...])
    for p in range(points):
        field[p] = tr_v[pl.ds(p, levels, stride=points), :]

    def table_of(ref):
        return halves(
            jnp.concatenate(
                [
                    jnp.concatenate([ref[EDGE_POINT[s][t]] for s in range(4)], axis=1)
                    for t in range(4)
                ],
                axis=0,
            )
        )

    def send_edges(table, turn):
        hi, lo = table
        sent = dot(hi, send_w[...]) + dot(lo, send_w[...])
        rest = jnp.zeros((3 * LANES - 4 * levels, LANES), F32)
        edge_out[turn] = jnp.concatenate([sent, rest], axis=0).T
        for copy in edge_copies(turn):
            copy.start()

    table = table_of(field)
    send_edges(table, 0)

    coef_rows = jnp.concatenate(
        [coef_v[:, i * LANES:(i + 1) * LANES] for i in range(src_tiles)], axis=0
    )
    coef_hi, coef_lo = halves(coef_rows)
    stack[:, 0:LANES] = coef_hi
    stack[:, LANES:2 * LANES] = coef_lo

    def wanted(pos_tile):
        pos = jnp.concatenate([pos_tile[k:k + 1, :] for k in range(per_tile)], axis=1).astype(I32)
        low = one_hot(iota((LANES, width), 0) == (pos & (LANES - 1)))
        high = pos >> 7
        all_tiles = dot(stack[...], jnp.concatenate([low, low], axis=0))
        got = jnp.zeros((levels, width), F32)
        for i in range(src_tiles):
            got = jnp.where(high == i, all_tiles[i * levels:(i + 1) * levels], got)
        return got

    def serve(d, carry):
        peer = lax.rem(dev + d, n_dev)
        pos_copy(peer, peer).wait_recv()
        blk_out[peer] = wanted(pos_in[peer])
        blk_copy(peer, dev).start()
        return carry

    lax.fori_loop(1, n_dev, serve, 0)
    blk_in[dev] = wanted(send_pos[pl.ds(pl.multiple_of(dev * 8, 8), 8), :])

    for s in range(4):
        nbr = nbr_v[s:s + 1, :]
        edge_w[:, s * LANES:(s + 1) * LANES] = one_hot(iota((5 * LANES, LANES), 0) == nbr)

    def gather_own(table):
        hi, lo = table
        weights = edge_w[0:4 * LANES, :]
        across_v[...] = dot(hi, weights) + dot(lo, weights)

    def gather_far(turn):
        for copy in edge_copies(turn):
            copy.wait_recv()
        hi, lo = halves(edge_in[turn].T[:4 * levels])
        weights = edge_w[4 * LANES:5 * LANES, :]
        across_v[...] += dot(hi, weights) + dot(lo, weights)

    def operator(ref, emit):
        scale = met_v[...]
        flips = [flip_v[s:s + 1, :] == 1 for s in range(4)]

        def chunk(i, carry):
            at = pl.multiple_of(i * 8, 8)
            u = [ref[p, pl.ds(at, 8), :] for p in range(points)]
            acc = [None] * points
            touch = [0] * points
            for s in range(4):
                for t in range(4):
                    p = EDGE_POINT[s][t]
                    lanes = slice(s * LANES, (s + 1) * LANES)
                    same = across_v[pl.ds(pl.multiple_of(t * levels + at, 8), 8), lanes]
                    back = across_v[pl.ds(pl.multiple_of((3 - t) * levels + at, 8), 8), lanes]
                    value = jnp.where(flips[s], back, same)
                    acc[p] = value if acc[p] is None else acc[p] + value
                    touch[p] += 1
            for p in range(points):
                total = None if acc[p] is None else PENALTY * acc[p]
                for q in range(points):
                    weight = lap[p, q] - (PENALTY * touch[p] if p == q else 0.0)
                    if weight != 0.0:
                        term = np.float32(weight) * u[q]
                        total = term if total is None else total + term
                emit(i, at, p, scale * total)
            return carry

        lax.fori_loop(0, levels // 8, chunk, 0)

    gather_own(table)
    gather_far(0)

    def keep_first(i, at, p, value):
        first[p, pl.ds(at, 8), :] = value

    operator(field, keep_first)
    table = table_of(first)
    send_edges(table, 1)
    gather_own(table)
    gather_far(1)

    def keep_stepped(i, at, p, value):
        lev_b[pl.ds(i * (8 * points) + p, 8, stride=points), :] = (
            field[p, pl.ds(at, 8), :] - HYPER * value
        )

    operator(first, keep_stepped)

    col_c[...] = jnp.zeros(col_c.shape, F32)

    def place_block(peer):
        rows = jnp.concatenate(
            [blk_in[peer, :, k * LANES:(k + 1) * LANES] for k in range(per_tile)], axis=0
        )
        both = jnp.concatenate(halves(rows), axis=1)
        for at in range(0, points, 2):
            lanes = slice(at * LANES, (at + 2) * LANES)
            spread = dot(both, spread_w[:, lanes])
            here = jnp.concatenate([tile[at:at + 1, :], tile[at + 1:at + 2, :]], axis=1)
            value = col_c[:, lanes]
            for k in range(per_tile):
                value = jnp.where(
                    here == peer * per_tile + k, spread[k * levels:(k + 1) * levels], value
                )
            col_c[:, lanes] = value

    place_block(dev)

    def take(d, carry):
        peer = lax.rem(dev + n_dev - d, n_dev)
        blk_copy(peer, peer).wait_recv()
        place_block(peer)
        return carry

    lax.fori_loop(1, n_dev, take, 0)
    for p in range(points):
        lev_c[pl.ds(p, levels, stride=points), :] = col_c[:, p * LANES:(p + 1) * LANES]

    def level(ref, k):
        return ref[pl.ds(pl.multiple_of(k * points, points), points), :]

    def put(ref, k, value):
        ref[pl.ds(pl.multiple_of(k * points, points), points), :] = value

    mid = levels // 2
    zero = jnp.zeros((points, LANES), F32)
    c_first = level(lev_c, 0)
    batch = 4

    def eliminate(step, carry):
        e, c_up, y, er, u, g, c_dn, z, gr, v = carry
        for part in range(batch):
            k = step * batch + part
            c1 = level(lev_c, k + 1)
            r = 1.0 / (e + c1)
            u = c1 * r
            y = (level(lev_b, k) + c_up * y) * r
            er = e * r
            e = 1.0 + c1 * er
            c_up = c1
            put(lev_u, k, u)
            put(lev_y, k, y)
            m = levels - 1 - k
            cm = level(lev_c, m)
            r = 1.0 / (g + cm)
            v = cm * r
            z = (level(lev_b, m) + c_dn * z) * r
            gr = g * r
            g = 1.0 + cm * gr
            c_dn = cm
            put(lev_u, m, v)
            put(lev_y, m, z)
        return e, c_up, y, er, u, g, c_dn, z, gr, v

    start = (1.0 + c_first, c_first, zero, zero, zero, zero + 1.0, zero, zero, zero, zero)
    e, c_up, y, er, u, g, c_dn, z, gr, v = lax.fori_loop(0, mid // batch, eliminate, start)
    x_top = (y + u * z) / (er + u * gr)
    x_bot = z + v * x_top
    put(out, mid - 1, x_top)
    put(out, mid, x_bot)

    def substitute(k, carry):
        x_up, x_dn = carry
        i = mid - 1 - k
        m = mid + k
        x_up = level(lev_y, i) + level(lev_u, i) * x_up
        x_dn = level(lev_y, m) + level(lev_u, m) * x_dn
        put(out, i, x_up)
        put(out, m, x_dn)
        return x_up, x_dn

    def substitute_batch(step, carry):
        for part in range(5):
            carry = substitute(1 + step * 5 + part, carry)
        return carry

    left = mid - 1
    carry = lax.fori_loop(0, left // 5, substitute_batch, (x_top, x_bot))
    for k in range(1 + left // 5 * 5, mid):
        carry = substitute(k, carry)

    def finish(d, carry):
        peer = lax.rem(dev + d, n_dev)
        pos_copy(peer, dev).wait_send()
        blk_copy(peer, dev).wait_send()
        return carry

    lax.fori_loop(1, n_dev, finish, 0)
    for turn in range(2):
        for copy in edge_copies(turn):
            copy.wait_send()


def on_device(n_grp, n_dev, tracer, metric, coef, nbr_slot, edge_flip, send_slot, span_slot):
    levels, points, elems = tracer.shape
    cols = coef.shape[1]
    width = max(cols // n_dev, LANES)
    rows = levels * points
    vmem = pltpu.VMEM
    dma = pltpu.SemaphoreType.DMA
    any_spec = pl.BlockSpec(memory_space=pl.ANY)
    mixed = pl.pallas_call(
        functools.partial(kernel, n_grp, n_dev, levels, cols),
        out_shape=jax.ShapeDtypeStruct((rows, elems), F32),
        in_specs=[any_spec] * 7,
        out_specs=pl.BlockSpec(memory_space=vmem),
        scratch_shapes=[
            vmem((rows, elems), F32),
            vmem((1, elems), F32),
            vmem((levels, cols), F32),
            vmem((4, elems), I32),
            vmem((4, elems), I32),
            vmem((1, 48), I32),
            vmem((points, elems), I32),
            vmem((n_dev * 8, LANES), F32),
            vmem((n_dev, 8, LANES), F32),
            vmem((cols // LANES * levels, 2 * LANES), BF16),
            vmem((n_dev, levels, width), F32),
            vmem((n_dev, levels, width), F32),
            vmem((2 * LANES, cols), BF16),
            vmem((5 * LANES, 4 * LANES), BF16),
            vmem((4 * LANES, LANES), BF16),
            vmem((2, LANES, 3 * LANES), F32),
            vmem((2, LANES, 3 * LANES), F32),
            vmem((4 * levels, 4 * LANES), F32),
            vmem((points, levels, elems), F32),
            vmem((points, levels, elems), F32),
            vmem((levels, cols), F32),
            vmem((rows, elems), F32),
            vmem((rows, elems), F32),
            vmem((rows, elems), F32),
            vmem((rows, elems), F32),
            dma((7,)),
            dma((n_dev,)),
            dma((n_dev,)),
            dma((n_dev,)),
            dma((n_dev,)),
            dma((2, 4)),
            dma((2, 4)),
        ],
        compiler_params=pltpu.CompilerParams(
            collective_id=0, has_side_effects=True, vmem_limit_bytes=40 * 2**20
        ),
        cost_estimate=pl.CostEstimate(flops=10**9, bytes_accessed=4 * 10**6, transcendentals=0),
        name="hyper_mix",
    )(
        tracer.reshape(rows, elems),
        metric.reshape(1, elems),
        coef,
        nbr_slot,
        edge_flip,
        send_slot.reshape(1, 48),
        span_slot,
    )
    return mixed.reshape(tracer.shape)


def solution(mesh):
    in_specs = (
        P(None, None, ("grp", "dev")),
        P(("grp", "dev")),
        P(None, ("grp", "dev")),
        P(None, ("grp", "dev")),
        P(None, ("grp", "dev")),
        P(("grp", "dev")),
        P(None, ("grp", "dev")),
    )
    out_specs = P(None, None, ("grp", "dev"))
    body = functools.partial(on_device, mesh.shape["grp"], mesh.shape["dev"])
    return jax.shard_map(body, mesh=mesh, in_specs=in_specs, out_specs=out_specs, check_vma=False)
```

```python
import functools

import jax
import jax.numpy as jnp
import numpy as np
from jax import lax
from jax.experimental import pallas as pl
from jax.experimental.pallas import tpu as pltpu
from jax.sharding import PartitionSpec as P

PENALTY = 10.0
HYPER = 0.0001
LANES = 128
MESH = pl.DeviceIdType.MESH
F32 = jnp.float32
BF16 = jnp.bfloat16
I32 = jnp.int32

EDGE_POINT = [[0, 1, 2, 3], [3, 7, 11, 15], [12, 13, 14, 15], [0, 4, 8, 12]]
EDGE_ROWS = [(0, 16, 1, 0), (16, 16, -1, 0), (32, 8, 0, 1), (40, 8, 0, -1)]


def gll_laplacian():
    gll_nodes = np.array([-1.0, -1.0 / np.sqrt(5.0), 1.0 / np.sqrt(5.0), 1.0])
    weights = np.array([1.0 / 6.0, 5.0 / 6.0, 5.0 / 6.0, 1.0 / 6.0])
    lambdas = np.ones(4)
    for jdx in range(4):
        for kdx in range(4):
            if kdx != jdx:
                lambdas[jdx] = lambdas[jdx] / (gll_nodes[jdx] - gll_nodes[kdx])
    derivative = np.zeros((4, 4))
    for idx in range(4):
        for jdx in range(4):
            if idx != jdx:
                derivative[idx, jdx] = (
                    lambdas[jdx] / lambdas[idx] / (gll_nodes[idx] - gll_nodes[jdx])
                )
        derivative[idx, idx] = -np.sum(derivative[idx])
    stiffness = -(derivative.T * weights[None, :] @ derivative) / weights[:, None]
    identity = np.eye(4)
    return np.kron(stiffness, identity) + np.kron(identity, stiffness)


def iota(shape, dim):
    return lax.broadcasted_iota(I32, shape, dim)


def one_hot(cond):
    return jnp.where(cond, 1.0, 0.0).astype(BF16)


def halves(value):
    hi = value.astype(BF16)
    lo = (value - hi.astype(F32)).astype(BF16)
    return hi, lo


def pick(value, lanes):
    return jnp.take_along_axis(value, lanes, axis=1, mode="promise_in_bounds")


def dot(a, b):
    return jnp.dot(a, b, preferred_element_type=F32)


def kernel(
    n_grp, n_dev, levels, cols,
    tr_h, met_h, coef_h, nbr_h, flip_h, send_h, span_h,
    out,
    tr_v, met_v, coef_v, nbr_v, flip_v, send_v, span_v,
    send_pos, pos_in, blk_out, blk_in, spread_w,
    edge_w, send_w, edge_out, edge_in, across_v,
    field, first, col_c, lev_c, lev_b, lev_u, lev_y,
    load_sem, pos_ssem, pos_rsem, blk_ssem, blk_rsem, edge_ssem, edge_rsem,
):
    grp, dev = lax.axis_index("grp"), lax.axis_index("dev")
    points = 16
    per_peer = cols // n_dev
    width = max(per_peer, LANES)
    per_tile = width // LANES
    src_tiles = cols // LANES
    lap = gll_laplacian()

    loads = [
        pltpu.make_async_copy(src, dst, load_sem.at[i])
        for i, (src, dst) in enumerate(
            [(span_h, span_v), (tr_h, tr_v), (send_h, send_v), (coef_h, coef_v),
             (nbr_h, nbr_v), (flip_h, flip_v), (met_h, met_v)]
        )
    ]
    for load in loads:
        load.start()

    barrier = pltpu.get_barrier_semaphore()
    for d in range(1, n_dev):
        pl.semaphore_signal(
            barrier, inc=1, device_id=(grp, lax.rem(dev + d, n_dev)), device_id_type=MESH
        )
    for step in (1, n_grp - 1):
        pl.semaphore_signal(
            barrier, inc=1, device_id=(lax.rem(grp + step, n_grp), dev), device_id_type=MESH
        )

    loads[0].wait()
    span = span_v[...]
    shift = cols.bit_length() - 1
    target = span >> shift
    place = span & (cols - 1)
    hits = jnp.concatenate(
        [jnp.where(target == r, 1.0, 0.0) for r in range(n_dev)], axis=0
    ).astype(BF16)
    count = n_dev * points
    before = one_hot(iota((LANES, LANES), 0) < iota((LANES, LANES), 1))
    along = dot(hits, before)
    totals = dot(hits, jnp.ones((LANES, LANES), BF16))
    row_i, col_i = iota((count, count), 0), iota((count, count), 1)
    earlier = one_hot((col_i < row_i) & ((col_i >> 4) == (row_i >> 4)))
    ranks = along + dot(earlier, totals.astype(BF16))
    rank = jnp.zeros((points, LANES), F32)
    for r in range(n_dev):
        rank = jnp.where(target == r, ranks[r * points:(r + 1) * points], rank)
    rank = rank.astype(I32)
    sub = rank >> 7
    lane = rank & (LANES - 1)
    tile = target * per_tile + sub
    row8 = target * 8 + sub
    place_hi = (place >> 7).astype(F32)
    place_lo = (place & (LANES - 1)).astype(F32)
    rows_out = n_dev * 8
    lists = []
    for p in range(points):
        spread_w[0:LANES, p * LANES:(p + 1) * LANES] = one_hot(
            iota((LANES, LANES), 0) == lane[p:p + 1, :]
        )
        mine = iota((rows_out, LANES), 0) == row8[p:p + 1, :]
        lists.append(
            jnp.concatenate(
                [jnp.where(mine, place_hi[p:p + 1, :], 0.0), jnp.where(mine, place_lo[p:p + 1, :], 0.0)],
                axis=0,
            ).astype(BF16)
        )
    packed = lax.dot_general(
        jnp.concatenate(lists, axis=1),
        spread_w[0:LANES, :],
        (((1,), (1,)), ((), ())),
        preferred_element_type=F32,
    )
    send_pos[...] = packed[:rows_out] * 128.0 + packed[rows_out:]
    edge_in[0, 48:LANES, :] = jnp.zeros((LANES - 48, 3 * LANES), F32)
    edge_in[1, 48:LANES, :] = jnp.zeros((LANES - 48, 3 * LANES), F32)
    send_w[...] = jnp.zeros(send_w.shape, BF16)

    pl.semaphore_wait(barrier, n_dev + 1)

    def pos_copy(peer, slot):
        return pltpu.make_async_remote_copy(
            src_ref=send_pos.at[pl.ds(pl.multiple_of(peer * 8, 8), 8), :],
            dst_ref=pos_in.at[slot],
            send_sem=pos_ssem.at[peer],
            recv_sem=pos_rsem.at[slot],
            device_id=(grp, peer),
            device_id_type=MESH,
        )

    def blk_copy(peer, slot):
        return pltpu.make_async_remote_copy(
            src_ref=blk_out.at[peer],
            dst_ref=blk_in.at[slot],
            send_sem=blk_ssem.at[peer],
            recv_sem=blk_rsem.at[slot],
            device_id=(grp, peer),
            device_id_type=MESH,
        )

    def edge_copies(turn):
        return [
            pltpu.make_async_remote_copy(
                src_ref=edge_out.at[turn, pl.ds(at, rows), :],
                dst_ref=edge_in.at[turn, pl.ds(at, rows), :],
                send_sem=edge_ssem.at[turn, k],
                recv_sem=edge_rsem.at[turn, k],
                device_id=(lax.rem(grp + n_grp + dg, n_grp), lax.rem(dev + n_dev + dv, n_dev)),
                device_id_type=MESH,
            )
            for k, (at, rows, dg, dv) in enumerate(EDGE_ROWS)
        ]

    def start_pos(d, carry):
        pos_copy(lax.rem(dev + d, n_dev), dev).start()
        return carry

    lax.fori_loop(1, n_dev, start_pos, 0)

    loads[1].wait()
    loads[2].wait()
    send_w[:, 0:48] = one_hot(iota((4 * LANES, 48), 0) == send_v[...])
    for p in range(points):
        field[p] = tr_v[pl.ds(p, levels, stride=points), :]

    def table_of(ref):
        return halves(
            jnp.concatenate(
                [
                    jnp.concatenate([ref[EDGE_POINT[s][t]] for s in range(4)], axis=1)
                    for t in range(4)
                ],
                axis=0,
            )
        )

    def send_edges(table, turn):
        hi, lo = table
        sent = dot(hi, send_w[...]) + dot(lo, send_w[...])
        rest = jnp.zeros((3 * LANES - 4 * levels, LANES), F32)
        edge_out[turn] = jnp.concatenate([sent, rest], axis=0).T
        for copy in edge_copies(turn):
            copy.start()

    table = table_of(field)
    send_edges(table, 0)

    loads[3].wait()

    def wanted(pos_tile, into):
        pos = pos_tile.astype(I32)
        for k in range(per_tile):
            here = jnp.broadcast_to(pos[k:k + 1, :], (8, LANES))
            low = here & (LANES - 1)
            high = here >> 7
            for at in range(0, levels, 8):
                got = pick(coef_v[at:at + 8, 0:LANES], low)
                for i in range(1, src_tiles):
                    other = pick(coef_v[at:at + 8, i * LANES:(i + 1) * LANES], low)
                    got = jnp.where(high == i, other, got)
                into[at:at + 8, k * LANES:(k + 1) * LANES] = got

    def serve(d, carry):
        peer = lax.rem(dev + d, n_dev)
        pos_copy(peer, peer).wait_recv()
        wanted(pos_in[peer], blk_out.at[peer])
        blk_copy(peer, dev).start()
        return carry

    lax.fori_loop(1, n_dev, serve, 0)
    wanted(send_pos[pl.ds(pl.multiple_of(dev * 8, 8), 8), :], blk_in.at[dev])

    for load in loads[4:]:
        load.wait()
    for s in range(4):
        nbr = nbr_v[s:s + 1, :]
        edge_w[:, s * LANES:(s + 1) * LANES] = one_hot(iota((5 * LANES, LANES), 0) == nbr)

    def gather_own(table):
        hi, lo = table
        weights = edge_w[0:4 * LANES, :]
        across_v[...] = dot(hi, weights) + dot(lo, weights)

    def gather_far(turn):
        for copy in edge_copies(turn):
            copy.wait_recv()
        hi, lo = halves(edge_in[turn].T[:4 * levels])
        weights = edge_w[4 * LANES:5 * LANES, :]
        across_v[...] += dot(hi, weights) + dot(lo, weights)

    def operator(ref, emit):
        scale = met_v[...]
        flips = [flip_v[s:s + 1, :] == 1 for s in range(4)]

        def chunk(i, carry):
            at = pl.multiple_of(i * 8, 8)
            u = [ref[p, pl.ds(at, 8), :] for p in range(points)]
            acc = [None] * points
            touch = [0] * points
            for s in range(4):
                for t in range(4):
                    p = EDGE_POINT[s][t]
                    lanes = slice(s * LANES, (s + 1) * LANES)
                    same = across_v[pl.ds(pl.multiple_of(t * levels + at, 8), 8), lanes]
                    back = across_v[pl.ds(pl.multiple_of((3 - t) * levels + at, 8), 8), lanes]
                    value = jnp.where(flips[s], back, same)
                    acc[p] = value if acc[p] is None else acc[p] + value
                    touch[p] += 1
            for p in range(points):
                total = None if acc[p] is None else PENALTY * acc[p]
                for q in range(points):
                    weight = lap[p, q] - (PENALTY * touch[p] if p == q else 0.0)
                    if weight != 0.0:
                        term = np.float32(weight) * u[q]
                        total = term if total is None else total + term
                emit(i, at, p, scale * total)
            return carry

        lax.fori_loop(0, levels // 8, chunk, 0)

    gather_own(table)
    gather_far(0)

    def keep_first(i, at, p, value):
        first[p, pl.ds(at, 8), :] = value

    operator(field, keep_first)
    table = table_of(first)
    send_edges(table, 1)
    gather_own(table)
    gather_far(1)

    def keep_stepped(i, at, p, value):
        lev_b[pl.ds(i * (8 * points) + p, 8, stride=points), :] = (
            field[p, pl.ds(at, 8), :] - HYPER * value
        )

    operator(first, keep_stepped)

    col_c[...] = jnp.zeros(col_c.shape, F32)

    def place_block(peer):
        for p in range(points):
            low = jnp.broadcast_to(lane[p:p + 1, :], (8, LANES))
            which = jnp.broadcast_to(tile[p:p + 1, :], (8, LANES)) - peer * per_tile
            masks = [which == k for k in range(per_tile)]
            for at in range(0, levels, 8):
                value = col_c[at:at + 8, p * LANES:(p + 1) * LANES]
                for k in range(per_tile):
                    other = pick(blk_in[peer, at:at + 8, k * LANES:(k + 1) * LANES], low)
                    value = jnp.where(masks[k], other, value)
                col_c[at:at + 8, p * LANES:(p + 1) * LANES] = value

    place_block(dev)

    def take(d, carry):
        peer = lax.rem(dev + n_dev - d, n_dev)
        blk_copy(peer, peer).wait_recv()
        place_block(peer)
        return carry

    lax.fori_loop(1, n_dev, take, 0)
    for p in range(points):
        lev_c[pl.ds(p, levels, stride=points), :] = col_c[:, p * LANES:(p + 1) * LANES]

    def level(ref, k):
        return ref[pl.ds(pl.multiple_of(k * points, points), points), :]

    def put(ref, k, value):
        ref[pl.ds(pl.multiple_of(k * points, points), points), :] = value

    mid = levels // 2
    zero = jnp.zeros((points, LANES), F32)
    c_first = level(lev_c, 0)
    batch = 4

    def eliminate(step, carry):
        e, c_up, y, er, u, g, c_dn, z, gr, v = carry
        for part in range(batch):
            k = step * batch + part
            c1 = level(lev_c, k + 1)
            r = pl.reciprocal(e + c1)
            u = c1 * r
            y = (level(lev_b, k) + c_up * y) * r
            er = e * r
            e = 1.0 + c1 * er
            c_up = c1
            put(lev_u, k, u)
            put(lev_y, k, y)
            m = levels - 1 - k
            cm = level(lev_c, m)
            r = pl.reciprocal(g + cm)
            v = cm * r
            z = (level(lev_b, m) + c_dn * z) * r
            gr = g * r
            g = 1.0 + cm * gr
            c_dn = cm
            put(lev_u, m, v)
            put(lev_y, m, z)
        return e, c_up, y, er, u, g, c_dn, z, gr, v

    start = (1.0 + c_first, c_first, zero, zero, zero, zero + 1.0, zero, zero, zero, zero)
    e, c_up, y, er, u, g, c_dn, z, gr, v = lax.fori_loop(0, mid // batch, eliminate, start)
    x_top = (y + u * z) / (er + u * gr)
    x_bot = z + v * x_top
    put(out, mid - 1, x_top)
    put(out, mid, x_bot)

    def substitute(k, carry):
        x_up, x_dn = carry
        i = mid - 1 - k
        m = mid + k
        x_up = level(lev_y, i) + level(lev_u, i) * x_up
        x_dn = level(lev_y, m) + level(lev_u, m) * x_dn
        put(out, i, x_up)
        put(out, m, x_dn)
        return x_up, x_dn

    def substitute_batch(step, carry):
        for part in range(5):
            carry = substitute(1 + step * 5 + part, carry)
        return carry

    left = mid - 1
    carry = lax.fori_loop(0, left // 5, substitute_batch, (x_top, x_bot))
    for k in range(1 + left // 5 * 5, mid):
        carry = substitute(k, carry)

    def finish(d, carry):
        peer = lax.rem(dev + d, n_dev)
        pos_copy(peer, dev).wait_send()
        blk_copy(peer, dev).wait_send()
        return carry

    lax.fori_loop(1, n_dev, finish, 0)
    for turn in range(2):
        for copy in edge_copies(turn):
            copy.wait_send()


def on_device(n_grp, n_dev, tracer, metric, coef, nbr_slot, edge_flip, send_slot, span_slot):
    levels, points, elems = tracer.shape
    cols = coef.shape[1]
    width = max(cols // n_dev, LANES)
    rows = levels * points
    vmem = pltpu.VMEM
    dma = pltpu.SemaphoreType.DMA
    any_spec = pl.BlockSpec(memory_space=pl.ANY)
    mixed = pl.pallas_call(
        functools.partial(kernel, n_grp, n_dev, levels, cols),
        out_shape=jax.ShapeDtypeStruct((rows, elems), F32),
        in_specs=[any_spec] * 7,
        out_specs=pl.BlockSpec(memory_space=vmem),
        scratch_shapes=[
            vmem((rows, elems), F32),
            vmem((1, elems), F32),
            vmem((levels, cols), F32),
            vmem((4, elems), I32),
            vmem((4, elems), I32),
            vmem((1, 48), I32),
            vmem((points, elems), I32),
            vmem((n_dev * 8, LANES), F32),
            vmem((n_dev, 8, LANES), F32),
            vmem((n_dev, levels, width), F32),
            vmem((n_dev, levels, width), F32),
            vmem((LANES, cols), BF16),
            vmem((5 * LANES, 4 * LANES), BF16),
            vmem((4 * LANES, LANES), BF16),
            vmem((2, LANES, 3 * LANES), F32),
            vmem((2, LANES, 3 * LANES), F32),
            vmem((4 * levels, 4 * LANES), F32),
            vmem((points, levels, elems), F32),
            vmem((points, levels, elems), F32),
            vmem((levels, cols), F32),
            vmem((rows, elems), F32),
            vmem((rows, elems), F32),
            vmem((rows, elems), F32),
            vmem((rows, elems), F32),
            dma((7,)),
            dma((n_dev,)),
            dma((n_dev,)),
            dma((n_dev,)),
            dma((n_dev,)),
            dma((2, 4)),
            dma((2, 4)),
        ],
        compiler_params=pltpu.CompilerParams(
            collective_id=0, has_side_effects=True, vmem_limit_bytes=62 * 2**20
        ),
        cost_estimate=pl.CostEstimate(flops=10**9, bytes_accessed=4 * 10**6, transcendentals=0),
        name="hyper_mix",
    )(
        tracer.reshape(rows, elems),
        metric.reshape(1, elems),
        coef,
        nbr_slot,
        edge_flip,
        send_slot.reshape(1, 48),
        span_slot,
    )
    return mixed.reshape(tracer.shape)


def solution(mesh):
    in_specs = (
        P(None, None, ("grp", "dev")),
        P(("grp", "dev")),
        P(None, ("grp", "dev")),
        P(None, ("grp", "dev")),
        P(None, ("grp", "dev")),
        P(("grp", "dev")),
        P(None, ("grp", "dev")),
    )
    out_specs = P(None, None, ("grp", "dev"))
    body = functools.partial(on_device, mesh.shape["grp"], mesh.shape["dev"])
    return jax.shard_map(body, mesh=mesh, in_specs=in_specs, out_specs=out_specs, check_vma=False)
```

```python
import functools

import jax
import jax.numpy as jnp
import numpy as np
from jax import lax
from jax.experimental import pallas as pl
from jax.experimental.pallas import tpu as pltpu
from jax.sharding import PartitionSpec as P

PENALTY = 10.0
HYPER = 0.0001
LANES = 128
MESH = pl.DeviceIdType.MESH
F32 = jnp.float32
BF16 = jnp.bfloat16
I32 = jnp.int32

EDGE_POINT = [[0, 1, 2, 3], [3, 7, 11, 15], [12, 13, 14, 15], [0, 4, 8, 12]]
EDGE_ROWS = [(0, 16, 1, 0), (16, 16, -1, 0), (32, 8, 0, 1), (40, 8, 0, -1)]


def gll_laplacian():
    gll_nodes = np.array([-1.0, -1.0 / np.sqrt(5.0), 1.0 / np.sqrt(5.0), 1.0])
    weights = np.array([1.0 / 6.0, 5.0 / 6.0, 5.0 / 6.0, 1.0 / 6.0])
    lambdas = np.ones(4)
    for jdx in range(4):
        for kdx in range(4):
            if kdx != jdx:
                lambdas[jdx] = lambdas[jdx] / (gll_nodes[jdx] - gll_nodes[kdx])
    derivative = np.zeros((4, 4))
    for idx in range(4):
        for jdx in range(4):
            if idx != jdx:
                derivative[idx, jdx] = (
                    lambdas[jdx] / lambdas[idx] / (gll_nodes[idx] - gll_nodes[jdx])
                )
        derivative[idx, idx] = -np.sum(derivative[idx])
    stiffness = -(derivative.T * weights[None, :] @ derivative) / weights[:, None]
    identity = np.eye(4)
    return np.kron(stiffness, identity) + np.kron(identity, stiffness)


def iota(shape, dim):
    return lax.broadcasted_iota(I32, shape, dim)


def one_hot(cond):
    return jnp.where(cond, 1.0, 0.0).astype(BF16)


def halves(value):
    hi = value.astype(BF16)
    lo = (value - hi.astype(F32)).astype(BF16)
    return hi, lo


def pick(value, lanes):
    return jnp.take_along_axis(value, lanes, axis=1, mode="promise_in_bounds")


def dot(a, b):
    return jnp.dot(a, b, preferred_element_type=F32)


def kernel(
    n_grp, n_dev, levels, cols,
    tr_h, met_h, coef_h, nbr_h, flip_h, send_h, span_h,
    lev_c, lev_b,
    tr_v, met_v, coef_v, nbr_v, flip_v, send_v, span_v,
    send_pos, pos_in, blk_out, blk_in, spread_w,
    edge_w, send_w, edge_out, edge_in, across_v,
    field, first, col_c,
    load_sem, pos_ssem, pos_rsem, blk_ssem, blk_rsem, edge_ssem, edge_rsem,
):
    grp, dev = lax.axis_index("grp"), lax.axis_index("dev")
    points = 16
    per_peer = cols // n_dev
    width = max(per_peer, LANES)
    per_tile = width // LANES
    src_tiles = cols // LANES
    lap = gll_laplacian()

    loads = [
        pltpu.make_async_copy(src, dst, load_sem.at[i])
        for i, (src, dst) in enumerate(
            [(span_h, span_v), (tr_h, tr_v), (send_h, send_v), (coef_h, coef_v),
             (nbr_h, nbr_v), (flip_h, flip_v), (met_h, met_v)]
        )
    ]
    for load in loads:
        load.start()

    barrier = pltpu.get_barrier_semaphore()
    for d in range(1, n_dev):
        pl.semaphore_signal(
            barrier, inc=1, device_id=(grp, lax.rem(dev + d, n_dev)), device_id_type=MESH
        )
    for step in (1, n_grp - 1):
        pl.semaphore_signal(
            barrier, inc=1, device_id=(lax.rem(grp + step, n_grp), dev), device_id_type=MESH
        )

    loads[0].wait()
    span = span_v[...]
    shift = cols.bit_length() - 1
    target = span >> shift
    place = span & (cols - 1)
    hits = jnp.concatenate(
        [jnp.where(target == r, 1.0, 0.0) for r in range(n_dev)], axis=0
    ).astype(BF16)
    count = n_dev * points
    before = one_hot(iota((LANES, LANES), 0) < iota((LANES, LANES), 1))
    along = dot(hits, before)
    totals = dot(hits, jnp.ones((LANES, LANES), BF16))
    row_i, col_i = iota((count, count), 0), iota((count, count), 1)
    earlier = one_hot((col_i < row_i) & ((col_i >> 4) == (row_i >> 4)))
    ranks = along + dot(earlier, totals.astype(BF16))
    rank = jnp.zeros((points, LANES), F32)
    for r in range(n_dev):
        rank = jnp.where(target == r, ranks[r * points:(r + 1) * points], rank)
    rank = rank.astype(I32)
    sub = rank >> 7
    lane = rank & (LANES - 1)
    tile = target * per_tile + sub
    row8 = target * 8 + sub
    place_hi = (place >> 7).astype(F32)
    place_lo = (place & (LANES - 1)).astype(F32)
    rows_out = n_dev * 8
    lists = []
    for p in range(points):
        spread_w[0:LANES, p * LANES:(p + 1) * LANES] = one_hot(
            iota((LANES, LANES), 0) == lane[p:p + 1, :]
        )
        mine = iota((rows_out, LANES), 0) == row8[p:p + 1, :]
        lists.append(
            jnp.concatenate(
                [jnp.where(mine, place_hi[p:p + 1, :], 0.0), jnp.where(mine, place_lo[p:p + 1, :], 0.0)],
                axis=0,
            ).astype(BF16)
        )
    packed = lax.dot_general(
        jnp.concatenate(lists, axis=1),
        spread_w[0:LANES, :],
        (((1,), (1,)), ((), ())),
        preferred_element_type=F32,
    )
    send_pos[...] = packed[:rows_out] * 128.0 + packed[rows_out:]
    edge_in[0, 48:LANES, :] = jnp.zeros((LANES - 48, 3 * LANES), F32)
    edge_in[1, 48:LANES, :] = jnp.zeros((LANES - 48, 3 * LANES), F32)
    send_w[...] = jnp.zeros(send_w.shape, BF16)

    pl.semaphore_wait(barrier, n_dev + 1)

    def pos_copy(peer, slot):
        return pltpu.make_async_remote_copy(
            src_ref=send_pos.at[pl.ds(pl.multiple_of(peer * 8, 8), 8), :],
            dst_ref=pos_in.at[slot],
            send_sem=pos_ssem.at[peer],
            recv_sem=pos_rsem.at[slot],
            device_id=(grp, peer),
            device_id_type=MESH,
        )

    def blk_copy(peer, slot):
        return pltpu.make_async_remote_copy(
            src_ref=blk_out.at[peer],
            dst_ref=blk_in.at[slot],
            send_sem=blk_ssem.at[peer],
            recv_sem=blk_rsem.at[slot],
            device_id=(grp, peer),
            device_id_type=MESH,
        )

    def edge_copies(turn):
        return [
            pltpu.make_async_remote_copy(
                src_ref=edge_out.at[turn, pl.ds(at, rows), :],
                dst_ref=edge_in.at[turn, pl.ds(at, rows), :],
                send_sem=edge_ssem.at[turn, k],
                recv_sem=edge_rsem.at[turn, k],
                device_id=(lax.rem(grp + n_grp + dg, n_grp), lax.rem(dev + n_dev + dv, n_dev)),
                device_id_type=MESH,
            )
            for k, (at, rows, dg, dv) in enumerate(EDGE_ROWS)
        ]

    def far(k):
        return n_dev // 2 + (1 - 2 * (k % 2)) * ((k + 1) // 2)

    def start_pos(k, carry):
        pos_copy(lax.rem(dev + n_dev - far(k), n_dev), dev).start()
        return carry

    lax.fori_loop(0, n_dev - 1, start_pos, 0)

    loads[1].wait()
    loads[2].wait()
    send_w[:, 0:48] = one_hot(iota((4 * LANES, 48), 0) == send_v[...])
    for p in range(points):
        field[p] = tr_v[pl.ds(p, levels, stride=points), :]

    def table_of(ref):
        return halves(
            jnp.concatenate(
                [
                    jnp.concatenate([ref[EDGE_POINT[s][t]] for s in range(4)], axis=1)
                    for t in range(4)
                ],
                axis=0,
            )
        )

    def send_edges(table, turn):
        hi, lo = table
        sent = dot(hi, send_w[...]) + dot(lo, send_w[...])
        rest = jnp.zeros((3 * LANES - 4 * levels, LANES), F32)
        edge_out[turn] = jnp.concatenate([sent, rest], axis=0).T
        for copy in edge_copies(turn):
            copy.start()

    table = table_of(field)
    send_edges(table, 0)

    loads[3].wait()

    def wanted(pos_tile, into):
        pos = pos_tile.astype(I32)
        for k in range(per_tile):
            here = jnp.broadcast_to(pos[k:k + 1, :], (8, LANES))
            low = here & (LANES - 1)
            high = here >> 7
            for at in range(0, levels, 8):
                got = pick(coef_v[at:at + 8, 0:LANES], low)
                for i in range(1, src_tiles):
                    other = pick(coef_v[at:at + 8, i * LANES:(i + 1) * LANES], low)
                    got = jnp.where(high == i, other, got)
                into[at:at + 8, k * LANES:(k + 1) * LANES] = got

    def serve(k, carry):
        peer = lax.rem(dev + far(k), n_dev)
        pos_copy(peer, peer).wait_recv()
        wanted(pos_in[peer], blk_out.at[peer])
        blk_copy(peer, dev).start()
        return carry

    lax.fori_loop(0, n_dev - 1, serve, 0)
    wanted(send_pos[pl.ds(pl.multiple_of(dev * 8, 8), 8), :], blk_in.at[dev])

    for load in loads[4:]:
        load.wait()
    for s in range(4):
        nbr = nbr_v[s:s + 1, :]
        edge_w[:, s * LANES:(s + 1) * LANES] = one_hot(iota((5 * LANES, LANES), 0) == nbr)

    def gather_own(table):
        hi, lo = table
        weights = edge_w[0:4 * LANES, :]
        across_v[...] = dot(hi, weights) + dot(lo, weights)

    def gather_far(turn):
        for copy in edge_copies(turn):
            copy.wait_recv()
        hi, lo = halves(edge_in[turn].T[:4 * levels])
        weights = edge_w[4 * LANES:5 * LANES, :]
        across_v[...] += dot(hi, weights) + dot(lo, weights)

    def operator(ref, emit):
        scale = met_v[...]
        flips = [flip_v[s:s + 1, :] == 1 for s in range(4)]

        def chunk(i, carry):
            at = pl.multiple_of(i * 8, 8)
            u = [ref[p, pl.ds(at, 8), :] for p in range(points)]
            acc = [None] * points
            touch = [0] * points
            for s in range(4):
                for t in range(4):
                    p = EDGE_POINT[s][t]
                    lanes = slice(s * LANES, (s + 1) * LANES)
                    same = across_v[pl.ds(pl.multiple_of(t * levels + at, 8), 8), lanes]
                    back = across_v[pl.ds(pl.multiple_of((3 - t) * levels + at, 8), 8), lanes]
                    value = jnp.where(flips[s], back, same)
                    acc[p] = value if acc[p] is None else acc[p] + value
                    touch[p] += 1
            for p in range(points):
                total = None if acc[p] is None else PENALTY * acc[p]
                for q in range(points):
                    weight = lap[p, q] - (PENALTY * touch[p] if p == q else 0.0)
                    if weight != 0.0:
                        term = np.float32(weight) * u[q]
                        total = term if total is None else total + term
                emit(i, at, p, scale * total)
            return carry

        lax.fori_loop(0, levels // 8, chunk, 0)

    gather_own(table)
    gather_far(0)

    def keep_first(i, at, p, value):
        first[p, pl.ds(at, 8), :] = value

    operator(field, keep_first)
    def arrived(k):
        peer = lax.rem(dev + n_dev - far(k), n_dev)
        blk_copy(peer, peer).wait_recv()
        return peer

    def place_blocks(peers, begin, last):
        for p in range(points):
            low = jnp.broadcast_to(lane[p:p + 1, :], (8, LANES))
            which = jnp.broadcast_to(tile[p:p + 1, :], (8, LANES))
            pairs = [(peer, k, which == peer * per_tile + k) for peer in peers for k in range(per_tile)]
            lanes = slice(p * LANES, (p + 1) * LANES)
            for at in range(0, levels, 8):
                value = None if begin else col_c[at:at + 8, lanes]
                for peer, k, mask in pairs:
                    other = pick(blk_in[peer, at:at + 8, k * LANES:(k + 1) * LANES], low)
                    value = other if value is None else jnp.where(mask, other, value)
                if last:
                    lev_c[pl.ds(at * points + p, 8, stride=points), :] = value
                else:
                    col_c[at:at + 8, lanes] = value

    table = table_of(first)
    send_edges(table, 1)
    gather_own(table)
    place_blocks([dev] + [arrived(k) for k in range(n_dev - 5)], True, False)
    gather_far(1)

    def keep_stepped(i, at, p, value):
        lev_b[pl.ds(i * (8 * points) + p, 8, stride=points), :] = (
            field[p, pl.ds(at, 8), :] - HYPER * value
        )

    operator(first, keep_stepped)
    place_blocks([arrived(k) for k in range(n_dev - 5, n_dev - 3)], False, False)
    place_blocks([arrived(k) for k in range(n_dev - 3, n_dev - 1)], False, True)

    def finish(d, carry):
        peer = lax.rem(dev + d, n_dev)
        pos_copy(peer, dev).wait_send()
        blk_copy(peer, dev).wait_send()
        return carry

    lax.fori_loop(1, n_dev, finish, 0)
    for turn in range(2):
        for copy in edge_copies(turn):
            copy.wait_send()


def solve_kernel(levels, lev_c, lev_b, out, out_v, lev_u, lev_y, sem):
    points = 16

    def level(ref, k):
        return ref[pl.ds(pl.multiple_of(k * points, points), points), :]

    def put(ref, k, value):
        ref[pl.ds(pl.multiple_of(k * points, points), points), :] = value

    mid = levels // 2
    zero = jnp.zeros((points, LANES), F32)
    c_first = level(lev_c, 0)
    batch = 4

    def eliminate(step, carry):
        e, c_up, y, er, u, g, c_dn, z, gr, v = carry
        for part in range(batch):
            k = step * batch + part
            c1 = level(lev_c, k + 1)
            r = pl.reciprocal(e + c1)
            u = c1 * r
            y = (level(lev_b, k) + c_up * y) * r
            er = e * r
            e = 1.0 + c1 * er
            c_up = c1
            put(lev_u, k, u)
            put(lev_y, k, y)
            m = levels - 1 - k
            cm = level(lev_c, m)
            r = pl.reciprocal(g + cm)
            v = cm * r
            z = (level(lev_b, m) + c_dn * z) * r
            gr = g * r
            g = 1.0 + cm * gr
            c_dn = cm
            put(lev_u, m, v)
            put(lev_y, m, z)
        return e, c_up, y, er, u, g, c_dn, z, gr, v

    start = (1.0 + c_first, c_first, zero, zero, zero, zero + 1.0, zero, zero, zero, zero)
    e, c_up, y, er, u, g, c_dn, z, gr, v = lax.fori_loop(0, mid // batch, eliminate, start)
    x_top = (y + u * z) / (er + u * gr)
    x_bot = z + v * x_top
    put(out_v, mid - 1, x_top)
    put(out_v, mid, x_bot)

    def substitute(k, carry):
        x_up, x_dn = carry
        i = mid - 1 - k
        m = mid + k
        x_up = level(lev_y, i) + level(lev_u, i) * x_up
        x_dn = level(lev_y, m) + level(lev_u, m) * x_dn
        put(out_v, i, x_up)
        put(out_v, m, x_dn)
        return x_up, x_dn

    copies = []

    def write(low, high):
        rows = pl.ds(low * points, (high - low) * points)
        copy = pltpu.make_async_copy(out_v.at[rows, :], out.at[rows, :], sem.at[len(copies)])
        copy.start()
        copies.append(copy)

    carry = (x_top, x_bot)
    done = 0
    for k in range(1, mid):
        carry = substitute(k, carry)
        if k % 6 == 5 or k == mid - 1:
            write(mid - 1 - k, mid - done)
            write(mid + done, mid + k + 1)
            done = k + 1
    for copy in copies:
        copy.wait()


def on_device(n_grp, n_dev, tracer, metric, coef, nbr_slot, edge_flip, send_slot, span_slot):
    levels, points, elems = tracer.shape
    cols = coef.shape[1]
    width = max(cols // n_dev, LANES)
    rows = levels * points
    vmem = pltpu.VMEM
    dma = pltpu.SemaphoreType.DMA
    hbm_spec = pl.BlockSpec(memory_space=pltpu.HBM)
    vmem_spec = pl.BlockSpec(memory_space=vmem)
    flat = jax.ShapeDtypeStruct((rows, elems), F32)
    mixing, stepped = pl.pallas_call(
        functools.partial(kernel, n_grp, n_dev, levels, cols),
        out_shape=[flat, flat],
        in_specs=[hbm_spec] * 7,
        out_specs=[vmem_spec, vmem_spec],
        scratch_shapes=[
            vmem((rows, elems), F32),
            vmem((1, elems), F32),
            vmem((levels, cols), F32),
            vmem((4, elems), I32),
            vmem((4, elems), I32),
            vmem((1, 48), I32),
            vmem((points, elems), I32),
            vmem((n_dev * 8, LANES), F32),
            vmem((n_dev, 8, LANES), F32),
            vmem((n_dev, levels, width), F32),
            vmem((n_dev, levels, width), F32),
            vmem((LANES, cols), BF16),
            vmem((5 * LANES, 4 * LANES), BF16),
            vmem((4 * LANES, LANES), BF16),
            vmem((2, LANES, 3 * LANES), F32),
            vmem((2, LANES, 3 * LANES), F32),
            vmem((4 * levels, 4 * LANES), F32),
            vmem((points, levels, elems), F32),
            vmem((points, levels, elems), F32),
            vmem((levels, cols), F32),
            dma((7,)),
            dma((n_dev,)),
            dma((n_dev,)),
            dma((n_dev,)),
            dma((n_dev,)),
            dma((2, 4)),
            dma((2, 4)),
        ],
        compiler_params=pltpu.CompilerParams(
            collective_id=0, has_side_effects=True, vmem_limit_bytes=40 * 2**20
        ),
        cost_estimate=pl.CostEstimate(flops=10**9, bytes_accessed=4 * 10**6, transcendentals=0),
        name="hyper_mix",
    )(
        *[
            pltpu.with_memory_space_constraint(array, pltpu.HBM)
            for array in (
                tracer.reshape(rows, elems),
                metric.reshape(1, elems),
                coef,
                nbr_slot,
                edge_flip,
                send_slot.reshape(1, 48),
                span_slot,
            )
        ]
    )
    mixed = pl.pallas_call(
        functools.partial(solve_kernel, levels),
        out_shape=flat,
        in_specs=[vmem_spec, vmem_spec],
        out_specs=hbm_spec,
        scratch_shapes=[vmem((rows, elems), F32)] * 3 + [dma((2 * (levels // 12 + 1),))],
        compiler_params=pltpu.CompilerParams(vmem_limit_bytes=40 * 2**20),
        cost_estimate=pl.CostEstimate(flops=10**7, bytes_accessed=2 * 10**6, transcendentals=0),
        name="column_solve",
    )(mixing, stepped)
    return mixed.reshape(tracer.shape)


def solution(mesh):
    in_specs = (
        P(None, None, ("grp", "dev")),
        P(("grp", "dev")),
        P(None, ("grp", "dev")),
        P(None, ("grp", "dev")),
        P(None, ("grp", "dev")),
        P(("grp", "dev")),
        P(None, ("grp", "dev")),
    )
    out_specs = P(None, None, ("grp", "dev"))
    body = functools.partial(on_device, mesh.shape["grp"], mesh.shape["dev"])
    return jax.shard_map(body, mesh=mesh, in_specs=in_specs, out_specs=out_specs, check_vma=False)
```

```python
import functools

import jax
import jax.numpy as jnp
import numpy as np
from jax import lax
from jax.experimental import pallas as pl
from jax.experimental.pallas import tpu as pltpu
from jax.sharding import PartitionSpec as P

PENALTY = 10.0
HYPER = 0.0001
LANES = 128
MESH = pl.DeviceIdType.MESH
F32 = jnp.float32
BF16 = jnp.bfloat16
I32 = jnp.int32

EDGE_POINT = [[0, 1, 2, 3], [3, 7, 11, 15], [12, 13, 14, 15], [0, 4, 8, 12]]
EDGE_ROWS = [(0, 16, 1, 0), (16, 16, -1, 0), (32, 8, 0, 1), (40, 8, 0, -1)]


def gll_laplacian():
    gll_nodes = np.array([-1.0, -1.0 / np.sqrt(5.0), 1.0 / np.sqrt(5.0), 1.0])
    weights = np.array([1.0 / 6.0, 5.0 / 6.0, 5.0 / 6.0, 1.0 / 6.0])
    lambdas = np.ones(4)
    for jdx in range(4):
        for kdx in range(4):
            if kdx != jdx:
                lambdas[jdx] = lambdas[jdx] / (gll_nodes[jdx] - gll_nodes[kdx])
    derivative = np.zeros((4, 4))
    for idx in range(4):
        for jdx in range(4):
            if idx != jdx:
                derivative[idx, jdx] = (
                    lambdas[jdx] / lambdas[idx] / (gll_nodes[idx] - gll_nodes[jdx])
                )
        derivative[idx, idx] = -np.sum(derivative[idx])
    stiffness = -(derivative.T * weights[None, :] @ derivative) / weights[:, None]
    identity = np.eye(4)
    return np.kron(stiffness, identity) + np.kron(identity, stiffness)


def iota(shape, dim):
    return lax.broadcasted_iota(I32, shape, dim)


def one_hot(cond):
    return jnp.where(cond, 1.0, 0.0).astype(BF16)


def halves(value):
    hi = value.astype(BF16)
    lo = (value - hi.astype(F32)).astype(BF16)
    return hi, lo


def pick(value, lanes):
    return jnp.take_along_axis(value, lanes, axis=1, mode="promise_in_bounds")


def dot(a, b):
    return jnp.dot(a, b, preferred_element_type=F32)


def kernel(
    n_grp, n_dev, levels, cols,
    tr_h, met_h, coef_h, nbr_h, flip_h, send_h, span_h,
    lev_c, lev_b,
    tr_v, met_v, coef_v, nbr_v, flip_v, send_v, span_v,
    send_pos, pos_in, blk_out, blk_in, spread_w,
    edge_w, send_w, edge_out, edge_in, across_v,
    field, first, col_c,
    load_sem, pos_ssem, pos_rsem, blk_ssem, blk_rsem, edge_ssem, edge_rsem,
):
    grp, dev = lax.axis_index("grp"), lax.axis_index("dev")
    points = 16
    per_peer = cols // n_dev
    width = max(per_peer, LANES)
    per_tile = width // LANES
    src_tiles = cols // LANES
    lap = gll_laplacian()

    loads = [
        pltpu.make_async_copy(src, dst, load_sem.at[i])
        for i, (src, dst) in enumerate(
            [(span_h, span_v), (tr_h, tr_v), (send_h, send_v), (coef_h, coef_v),
             (nbr_h, nbr_v), (flip_h, flip_v), (met_h, met_v)]
        )
    ]
    for load in loads:
        load.start()

    barrier = pltpu.get_barrier_semaphore()
    for d in range(1, n_dev):
        pl.semaphore_signal(
            barrier, inc=1, device_id=(grp, lax.rem(dev + d, n_dev)), device_id_type=MESH
        )
    for step in (1, n_grp - 1):
        pl.semaphore_signal(
            barrier, inc=1, device_id=(lax.rem(grp + step, n_grp), dev), device_id_type=MESH
        )

    loads[0].wait()
    span = span_v[...]
    shift = cols.bit_length() - 1
    target = span >> shift
    place = span & (cols - 1)
    hits = jnp.concatenate(
        [jnp.where(target == r, 1.0, 0.0) for r in range(n_dev)], axis=0
    ).astype(BF16)
    count = n_dev * points
    before = one_hot(iota((LANES, LANES), 0) < iota((LANES, LANES), 1))
    along = dot(hits, before)
    totals = dot(hits, jnp.ones((LANES, LANES), BF16))
    row_i, col_i = iota((count, count), 0), iota((count, count), 1)
    earlier = one_hot((col_i < row_i) & ((col_i >> 4) == (row_i >> 4)))
    ranks = along + dot(earlier, totals.astype(BF16))
    rank = jnp.zeros((points, LANES), F32)
    for r in range(n_dev):
        rank = jnp.where(target == r, ranks[r * points:(r + 1) * points], rank)
    rank = rank.astype(I32)
    sub = rank >> 7
    lane = rank & (LANES - 1)
    tile = target * per_tile + sub
    row8 = target * 8 + sub
    place_hi = (place >> 7).astype(F32)
    place_lo = (place & (LANES - 1)).astype(F32)
    rows_out = n_dev * 8
    lists = []
    for p in range(points):
        spread_w[0:LANES, p * LANES:(p + 1) * LANES] = one_hot(
            iota((LANES, LANES), 0) == lane[p:p + 1, :]
        )
        mine = iota((rows_out, LANES), 0) == row8[p:p + 1, :]
        lists.append(
            jnp.concatenate(
                [jnp.where(mine, place_hi[p:p + 1, :], 0.0), jnp.where(mine, place_lo[p:p + 1, :], 0.0)],
                axis=0,
            ).astype(BF16)
        )
    packed = lax.dot_general(
        jnp.concatenate(lists, axis=1),
        spread_w[0:LANES, :],
        (((1,), (1,)), ((), ())),
        preferred_element_type=F32,
    )
    send_pos[...] = packed[:rows_out] * 128.0 + packed[rows_out:]
    edge_in[0, 48:LANES, :] = jnp.zeros((LANES - 48, 3 * LANES), F32)
    edge_in[1, 48:LANES, :] = jnp.zeros((LANES - 48, 3 * LANES), F32)
    send_w[...] = jnp.zeros(send_w.shape, BF16)

    pl.semaphore_wait(barrier, n_dev + 1)

    def pos_copy(peer, slot):
        return pltpu.make_async_remote_copy(
            src_ref=send_pos.at[pl.ds(pl.multiple_of(peer * 8, 8), 8), :],
            dst_ref=pos_in.at[slot],
            send_sem=pos_ssem.at[peer],
            recv_sem=pos_rsem.at[slot],
            device_id=(grp, peer),
            device_id_type=MESH,
        )

    def blk_copy(peer, slot):
        return pltpu.make_async_remote_copy(
            src_ref=blk_out.at[peer],
            dst_ref=blk_in.at[slot],
            send_sem=blk_ssem.at[peer],
            recv_sem=blk_rsem.at[slot],
            device_id=(grp, peer),
            device_id_type=MESH,
        )

    def edge_copies(turn):
        return [
            pltpu.make_async_remote_copy(
                src_ref=edge_out.at[turn, pl.ds(at, rows), :],
                dst_ref=edge_in.at[turn, pl.ds(at, rows), :],
                send_sem=edge_ssem.at[turn, k],
                recv_sem=edge_rsem.at[turn, k],
                device_id=(lax.rem(grp + n_grp + dg, n_grp), lax.rem(dev + n_dev + dv, n_dev)),
                device_id_type=MESH,
            )
            for k, (at, rows, dg, dv) in enumerate(EDGE_ROWS)
        ]

    def far(k):
        return n_dev // 2 + (1 - 2 * (k % 2)) * ((k + 1) // 2)

    def start_pos(k, carry):
        pos_copy(lax.rem(dev + n_dev - far(k), n_dev), dev).start()
        return carry

    lax.fori_loop(0, n_dev - 1, start_pos, 0)

    for load in loads[1:]:
        load.wait()
    send_w[:, 0:48] = one_hot(iota((4 * LANES, 48), 0) == send_v[...])
    for p in range(points):
        field[p] = tr_v[pl.ds(p, levels, stride=points), :]

    def table_of(ref):
        return halves(
            jnp.concatenate(
                [
                    jnp.concatenate([ref[EDGE_POINT[s][t]] for s in range(4)], axis=1)
                    for t in range(4)
                ],
                axis=0,
            )
        )

    def send_edges(table, turn):
        hi, lo = table
        sent = dot(hi, send_w[...]) + dot(lo, send_w[...])
        rest = jnp.zeros((3 * LANES - 4 * levels, LANES), F32)
        edge_out[turn] = jnp.concatenate([sent, rest], axis=0).T
        for copy in edge_copies(turn):
            copy.start()

    table = table_of(field)
    send_edges(table, 0)

    def wanted(pos, into, at):
        for k in range(per_tile):
            here = jnp.broadcast_to(pos[k:k + 1, :], (8, LANES))
            low = here & (LANES - 1)
            high = here >> 7
            got = pick(coef_v[pl.ds(at, 8), 0:LANES], low)
            for i in range(1, src_tiles):
                other = pick(coef_v[pl.ds(at, 8), i * LANES:(i + 1) * LANES], low)
                got = jnp.where(high == i, other, got)
            into[pl.ds(at, 8), k * LANES:(k + 1) * LANES] = got

    def serve(k, carry):
        peer = lax.rem(dev + far(k), n_dev)
        pos_copy(peer, peer).wait_recv()
        pos = pos_in[peer].astype(I32)
        for at in range(0, levels, 8):
            wanted(pos, blk_out.at[peer], at)
        blk_copy(peer, dev).start()
        return carry

    lax.fori_loop(0, n_dev - 1, serve, 0)

    for s in range(4):
        nbr = nbr_v[s:s + 1, :]
        edge_w[:, s * LANES:(s + 1) * LANES] = one_hot(iota((5 * LANES, LANES), 0) == nbr)

    def gather_own(table):
        hi, lo = table
        weights = edge_w[0:4 * LANES, :]
        across_v[...] = dot(hi, weights) + dot(lo, weights)

    def gather_far(turn):
        for copy in edge_copies(turn):
            copy.wait_recv()
        hi, lo = halves(edge_in[turn].T[:4 * levels])
        weights = edge_w[4 * LANES:5 * LANES, :]
        across_v[...] += dot(hi, weights) + dot(lo, weights)

    def operator(ref, emit, beside):
        scale = met_v[...]
        flips = [flip_v[s:s + 1, :] == 1 for s in range(4)]

        def chunk(i):
            at = pl.multiple_of(i * 8, 8)
            beside(at)
            u = [ref[p, pl.ds(at, 8), :] for p in range(points)]
            acc = [None] * points
            touch = [0] * points
            for s in range(4):
                for t in range(4):
                    p = EDGE_POINT[s][t]
                    lanes = slice(s * LANES, (s + 1) * LANES)
                    same = across_v[pl.ds(pl.multiple_of(t * levels + at, 8), 8), lanes]
                    back = across_v[pl.ds(pl.multiple_of((3 - t) * levels + at, 8), 8), lanes]
                    value = jnp.where(flips[s], back, same)
                    acc[p] = value if acc[p] is None else acc[p] + value
                    touch[p] += 1
            for p in range(points):
                total = None if acc[p] is None else PENALTY * acc[p]
                for q in range(points):
                    weight = lap[p, q] - (PENALTY * touch[p] if p == q else 0.0)
                    if weight != 0.0:
                        term = np.float32(weight) * u[q]
                        total = term if total is None else total + term
                emit(i, at, p, scale * total)

        def chunks(step, carry):
            for part in range(3):
                chunk(step * 3 + part)
            return carry

        lax.fori_loop(0, levels // 24, chunks, 0)

    gather_own(table)
    gather_far(0)

    def keep_first(i, at, p, value):
        first[p, pl.ds(at, 8), :] = value

    own_pos = send_pos[pl.ds(pl.multiple_of(dev * 8, 8), 8), :].astype(I32)
    operator(field, keep_first, lambda at: wanted(own_pos, blk_in.at[dev], at))
    def arrived(k):
        peer = lax.rem(dev + n_dev - far(k), n_dev)
        blk_copy(peer, peer).wait_recv()
        return peer

    def place_blocks(peers, begin, last, at):
        for p in range(points):
            low = jnp.broadcast_to(lane[p:p + 1, :], (8, LANES))
            which = jnp.broadcast_to(tile[p:p + 1, :], (8, LANES))
            lanes = slice(p * LANES, (p + 1) * LANES)
            value = None if begin else col_c[pl.ds(at, 8), lanes]
            for peer in peers:
                for k in range(per_tile):
                    other = pick(blk_in[peer, pl.ds(at, 8), k * LANES:(k + 1) * LANES], low)
                    mask = which == peer * per_tile + k
                    value = other if value is None else jnp.where(mask, other, value)
            if last:
                lev_c[pl.ds(at * points + p, 8, stride=points), :] = value
            else:
                col_c[pl.ds(at, 8), lanes] = value

    table = table_of(first)
    send_edges(table, 1)
    peers = [dev] + [arrived(k) for k in range(n_dev - 5)]
    gather_own(table)
    for at in range(0, levels, 8):
        place_blocks(peers, True, False, at)
    gather_far(1)

    def keep_stepped(i, at, p, value):
        lev_b[pl.ds(i * (8 * points) + p, 8, stride=points), :] = (
            field[p, pl.ds(at, 8), :] - HYPER * value
        )

    nearer = [arrived(k) for k in range(n_dev - 5, n_dev - 3)]
    operator(first, keep_stepped, lambda at: place_blocks(nearer, False, False, at))
    nearest = [arrived(k) for k in range(n_dev - 3, n_dev - 1)]
    for at in range(0, levels, 8):
        place_blocks(nearest, False, True, at)

    def finish(d, carry):
        peer = lax.rem(dev + d, n_dev)
        pos_copy(peer, dev).wait_send()
        blk_copy(peer, dev).wait_send()
        return carry

    lax.fori_loop(1, n_dev, finish, 0)
    for turn in range(2):
        for copy in edge_copies(turn):
            copy.wait_send()


def solve_kernel(levels, lev_c, lev_b, out, out_v, lev_u, lev_y, sem):
    points = 16

    def level(ref, k):
        return ref[pl.ds(pl.multiple_of(k * points, points), points), :]

    def put(ref, k, value):
        ref[pl.ds(pl.multiple_of(k * points, points), points), :] = value

    mid = levels // 2
    zero = jnp.zeros((points, LANES), F32)
    c_first = level(lev_c, 0)
    batch = 4

    def eliminate(step, carry):
        e, c_up, y, er, u, g, c_dn, z, gr, v = carry
        for part in range(batch):
            k = step * batch + part
            c1 = level(lev_c, k + 1)
            r = pl.reciprocal(e + c1)
            u = c1 * r
            y = (level(lev_b, k) + c_up * y) * r
            er = e * r
            e = 1.0 + c1 * er
            c_up = c1
            put(lev_u, k, u)
            put(lev_y, k, y)
            m = levels - 1 - k
            cm = level(lev_c, m)
            r = pl.reciprocal(g + cm)
            v = cm * r
            z = (level(lev_b, m) + c_dn * z) * r
            gr = g * r
            g = 1.0 + cm * gr
            c_dn = cm
            put(lev_u, m, v)
            put(lev_y, m, z)
        return e, c_up, y, er, u, g, c_dn, z, gr, v

    start = (1.0 + c_first, c_first, zero, zero, zero, zero + 1.0, zero, zero, zero, zero)
    e, c_up, y, er, u, g, c_dn, z, gr, v = lax.fori_loop(0, mid // batch, eliminate, start)
    x_top = (y + u * z) / (er + u * gr)
    x_bot = z + v * x_top
    put(out_v, mid - 1, x_top)
    put(out_v, mid, x_bot)

    def substitute(k, carry):
        x_up, x_dn = carry
        i = mid - 1 - k
        m = mid + k
        x_up = level(lev_y, i) + level(lev_u, i) * x_up
        x_dn = level(lev_y, m) + level(lev_u, m) * x_dn
        put(out_v, i, x_up)
        put(out_v, m, x_dn)
        return x_up, x_dn

    copies = []

    def write(low, high):
        rows = pl.ds(low * points, (high - low) * points)
        copy = pltpu.make_async_copy(out_v.at[rows, :], out.at[rows, :], sem.at[len(copies)])
        copy.start()
        copies.append(copy)

    carry = (x_top, x_bot)
    done = 0
    for k in range(1, mid):
        carry = substitute(k, carry)
        if k % 6 == 5 or k == mid - 1:
            write(mid - 1 - k, mid - done)
            write(mid + done, mid + k + 1)
            done = k + 1
    for copy in copies:
        copy.wait()


def on_device(n_grp, n_dev, tracer, metric, coef, nbr_slot, edge_flip, send_slot, span_slot):
    levels, points, elems = tracer.shape
    cols = coef.shape[1]
    width = max(cols // n_dev, LANES)
    rows = levels * points
    vmem = pltpu.VMEM
    dma = pltpu.SemaphoreType.DMA
    hbm_spec = pl.BlockSpec(memory_space=pltpu.HBM)
    vmem_spec = pl.BlockSpec(memory_space=vmem)
    flat = jax.ShapeDtypeStruct((rows, elems), F32)
    mixing, stepped = pl.pallas_call(
        functools.partial(kernel, n_grp, n_dev, levels, cols),
        out_shape=[flat, flat],
        in_specs=[hbm_spec] * 7,
        out_specs=[vmem_spec, vmem_spec],
        scratch_shapes=[
            vmem((rows, elems), F32),
            vmem((1, elems), F32),
            vmem((levels, cols), F32),
            vmem((4, elems), I32),
            vmem((4, elems), I32),
            vmem((1, 48), I32),
            vmem((points, elems), I32),
            vmem((n_dev * 8, LANES), F32),
            vmem((n_dev, 8, LANES), F32),
            vmem((n_dev, levels, width), F32),
            vmem((n_dev, levels, width), F32),
            vmem((LANES, cols), BF16),
            vmem((5 * LANES, 4 * LANES), BF16),
            vmem((4 * LANES, LANES), BF16),
            vmem((2, LANES, 3 * LANES), F32),
            vmem((2, LANES, 3 * LANES), F32),
            vmem((4 * levels, 4 * LANES), F32),
            vmem((points, levels, elems), F32),
            vmem((points, levels, elems), F32),
            vmem((levels, cols), F32),
            dma((7,)),
            dma((n_dev,)),
            dma((n_dev,)),
            dma((n_dev,)),
            dma((n_dev,)),
            dma((2, 4)),
            dma((2, 4)),
        ],
        compiler_params=pltpu.CompilerParams(
            collective_id=0, has_side_effects=True, vmem_limit_bytes=40 * 2**20
        ),
        cost_estimate=pl.CostEstimate(flops=10**9, bytes_accessed=4 * 10**6, transcendentals=0),
        name="hyper_mix",
    )(
        *[
            pltpu.with_memory_space_constraint(array, pltpu.HBM)
            for array in (
                tracer.reshape(rows, elems),
                metric.reshape(1, elems),
                coef,
                nbr_slot,
                edge_flip,
                send_slot.reshape(1, 48),
                span_slot,
            )
        ]
    )
    mixed = pl.pallas_call(
        functools.partial(solve_kernel, levels),
        out_shape=flat,
        in_specs=[vmem_spec, vmem_spec],
        out_specs=hbm_spec,
        scratch_shapes=[vmem((rows, elems), F32)] * 3 + [dma((2 * (levels // 12 + 1),))],
        compiler_params=pltpu.CompilerParams(vmem_limit_bytes=40 * 2**20),
        cost_estimate=pl.CostEstimate(flops=10**7, bytes_accessed=2 * 10**6, transcendentals=0),
        name="column_solve",
    )(mixing, stepped)
    return mixed.reshape(tracer.shape)


def solution(mesh):
    in_specs = (
        P(None, None, ("grp", "dev")),
        P(("grp", "dev")),
        P(None, ("grp", "dev")),
        P(None, ("grp", "dev")),
        P(None, ("grp", "dev")),
        P(("grp", "dev")),
        P(None, ("grp", "dev")),
    )
    out_specs = P(None, None, ("grp", "dev"))
    body = functools.partial(on_device, mesh.shape["grp"], mesh.shape["dev"])
    return jax.shard_map(body, mesh=mesh, in_specs=in_specs, out_specs=out_specs, check_vma=False)
```

```python
import functools

import jax
import jax.numpy as jnp
import numpy as np
from jax import lax
from jax.experimental import pallas as pl
from jax.experimental.pallas import tpu as pltpu
from jax.sharding import PartitionSpec as P

PENALTY = 10.0
HYPER = 0.0001
LANES = 128
MESH = pl.DeviceIdType.MESH
F32 = jnp.float32
BF16 = jnp.bfloat16
I32 = jnp.int32

EDGE_POINT = [[0, 1, 2, 3], [3, 7, 11, 15], [12, 13, 14, 15], [0, 4, 8, 12]]
EDGE_ROWS = [(0, 16, 1, 0), (16, 16, -1, 0), (32, 8, 0, 1), (40, 8, 0, -1)]


def gll_laplacian():
    gll_nodes = np.array([-1.0, -1.0 / np.sqrt(5.0), 1.0 / np.sqrt(5.0), 1.0])
    weights = np.array([1.0 / 6.0, 5.0 / 6.0, 5.0 / 6.0, 1.0 / 6.0])
    lambdas = np.ones(4)
    for jdx in range(4):
        for kdx in range(4):
            if kdx != jdx:
                lambdas[jdx] = lambdas[jdx] / (gll_nodes[jdx] - gll_nodes[kdx])
    derivative = np.zeros((4, 4))
    for idx in range(4):
        for jdx in range(4):
            if idx != jdx:
                derivative[idx, jdx] = (
                    lambdas[jdx] / lambdas[idx] / (gll_nodes[idx] - gll_nodes[jdx])
                )
        derivative[idx, idx] = -np.sum(derivative[idx])
    stiffness = -(derivative.T * weights[None, :] @ derivative) / weights[:, None]
    identity = np.eye(4)
    return np.kron(stiffness, identity) + np.kron(identity, stiffness)


def iota(shape, dim):
    return lax.broadcasted_iota(I32, shape, dim)


def one_hot(cond):
    return jnp.where(cond, 1.0, 0.0).astype(BF16)


def halves(value):
    hi = value.astype(BF16)
    lo = (value - hi.astype(F32)).astype(BF16)
    return hi, lo


def pick(value, lanes):
    return jnp.take_along_axis(value, lanes, axis=1, mode="promise_in_bounds")


def dot(a, b):
    return jnp.dot(a, b, preferred_element_type=F32)


def kernel(
    n_grp, n_dev, levels, cols,
    tr_h, met_h, coef_h, nbr_h, flip_h, send_h, span_h,
    lev_c, lev_b,
    tr_v, met_v, coef_v, nbr_v, flip_v, send_v, span_v,
    send_pos, pos_in, stack, blk_out, blk_in, spread_w,
    edge_w, send_w, edge_out, edge_in, across_v,
    field, first, col_c,
    load_sem, pos_ssem, pos_rsem, blk_ssem, blk_rsem, edge_ssem, edge_rsem,
):
    grp, dev = lax.axis_index("grp"), lax.axis_index("dev")
    points = 16
    per_peer = cols // n_dev
    width = max(per_peer, LANES)
    per_tile = width // LANES
    src_tiles = cols // LANES
    lap = gll_laplacian()

    loads = [
        pltpu.make_async_copy(src, dst, load_sem.at[i])
        for i, (src, dst) in enumerate(
            [(span_h, span_v), (tr_h, tr_v), (send_h, send_v), (coef_h, coef_v),
             (nbr_h, nbr_v), (flip_h, flip_v), (met_h, met_v)]
        )
    ]
    for load in loads:
        load.start()

    barrier = pltpu.get_barrier_semaphore()
    for d in range(1, n_dev):
        pl.semaphore_signal(
            barrier, inc=1, device_id=(grp, lax.rem(dev + d, n_dev)), device_id_type=MESH
        )
    for step in (1, n_grp - 1):
        pl.semaphore_signal(
            barrier, inc=1, device_id=(lax.rem(grp + step, n_grp), dev), device_id_type=MESH
        )

    loads[0].wait()
    span = span_v[...]
    shift = cols.bit_length() - 1
    target = span >> shift
    place = span & (cols - 1)
    hits = jnp.concatenate(
        [jnp.where(target == r, 1.0, 0.0) for r in range(n_dev)], axis=0
    ).astype(BF16)
    count = n_dev * points
    before = one_hot(iota((LANES, LANES), 0) < iota((LANES, LANES), 1))
    along = dot(hits, before)
    totals = dot(hits, jnp.ones((LANES, LANES), BF16))
    row_i, col_i = iota((count, count), 0), iota((count, count), 1)
    earlier = one_hot((col_i < row_i) & ((col_i >> 4) == (row_i >> 4)))
    ranks = along + dot(earlier, totals.astype(BF16))
    rank = jnp.zeros((points, LANES), F32)
    for r in range(n_dev):
        rank = jnp.where(target == r, ranks[r * points:(r + 1) * points], rank)
    rank = rank.astype(I32)
    sub = rank >> 7
    lane = rank & (LANES - 1)
    tile = target * per_tile + sub
    row8 = target * 8 + sub
    place_hi = (place >> 7).astype(F32)
    place_lo = (place & (LANES - 1)).astype(F32)
    rows_out = n_dev * 8
    lists = []
    for p in range(points):
        spread_w[0:LANES, p * LANES:(p + 1) * LANES] = one_hot(
            iota((LANES, LANES), 0) == lane[p:p + 1, :]
        )
        mine = iota((rows_out, LANES), 0) == row8[p:p + 1, :]
        lists.append(
            jnp.concatenate(
                [jnp.where(mine, place_hi[p:p + 1, :], 0.0), jnp.where(mine, place_lo[p:p + 1, :], 0.0)],
                axis=0,
            ).astype(BF16)
        )
    packed = lax.dot_general(
        jnp.concatenate(lists, axis=1),
        spread_w[0:LANES, :],
        (((1,), (1,)), ((), ())),
        preferred_element_type=F32,
    )
    send_pos[...] = packed[:rows_out] * 128.0 + packed[rows_out:]
    edge_in[0, 48:LANES, :] = jnp.zeros((LANES - 48, 3 * LANES), F32)
    edge_in[1, 48:LANES, :] = jnp.zeros((LANES - 48, 3 * LANES), F32)
    send_w[...] = jnp.zeros(send_w.shape, BF16)

    pl.semaphore_wait(barrier, n_dev + 1)

    def pos_copy(peer, slot):
        return pltpu.make_async_remote_copy(
            src_ref=send_pos.at[pl.ds(pl.multiple_of(peer * 8, 8), 8), :],
            dst_ref=pos_in.at[slot],
            send_sem=pos_ssem.at[peer],
            recv_sem=pos_rsem.at[slot],
            device_id=(grp, peer),
            device_id_type=MESH,
        )

    def blk_copy(peer, slot):
        return pltpu.make_async_remote_copy(
            src_ref=blk_out.at[peer],
            dst_ref=blk_in.at[slot],
            send_sem=blk_ssem.at[peer],
            recv_sem=blk_rsem.at[slot],
            device_id=(grp, peer),
            device_id_type=MESH,
        )

    def edge_copies(turn):
        return [
            pltpu.make_async_remote_copy(
                src_ref=edge_out.at[turn, pl.ds(at, rows), :],
                dst_ref=edge_in.at[turn, pl.ds(at, rows), :],
                send_sem=edge_ssem.at[turn, k],
                recv_sem=edge_rsem.at[turn, k],
                device_id=(lax.rem(grp + n_grp + dg, n_grp), lax.rem(dev + n_dev + dv, n_dev)),
                device_id_type=MESH,
            )
            for k, (at, rows, dg, dv) in enumerate(EDGE_ROWS)
        ]

    def far(k):
        return n_dev // 2 + (1 - 2 * (k % 2)) * ((k + 1) // 2)

    def start_pos(k, carry):
        pos_copy(lax.rem(dev + n_dev - far(k), n_dev), dev).start()
        return carry

    lax.fori_loop(0, n_dev - 1, start_pos, 0)

    loads[1].wait()
    loads[2].wait()
    send_w[:, 0:48] = one_hot(iota((4 * LANES, 48), 0) == send_v[...])
    for p in range(points):
        field[p] = tr_v[pl.ds(p, levels, stride=points), :]

    def table_of(ref):
        return halves(
            jnp.concatenate(
                [
                    jnp.concatenate([ref[EDGE_POINT[s][t]] for s in range(4)], axis=1)
                    for t in range(4)
                ],
                axis=0,
            )
        )

    def send_edges(table, turn):
        hi, lo = table
        sent = dot(hi, send_w[...]) + dot(lo, send_w[...])
        rest = jnp.zeros((3 * LANES - 4 * levels, LANES), F32)
        edge_out[turn] = jnp.concatenate([sent, rest], axis=0).T
        for copy in edge_copies(turn):
            copy.start()

    table = table_of(field)
    send_edges(table, 0)

    loads[3].wait()

    by_dot = levels // 2 // 16 * 16
    coef_hi, coef_lo = halves(
        jnp.concatenate(
            [coef_v[0:by_dot, i * LANES:(i + 1) * LANES] for i in range(src_tiles)], axis=0
        )
    )
    stack[:, 0:LANES] = coef_hi
    stack[:, LANES:2 * LANES] = coef_lo

    def wanted(pos_tile, into):
        pos = pos_tile.astype(I32)
        row = jnp.concatenate([pos[k:k + 1, :] for k in range(per_tile)], axis=1)
        chosen = one_hot(iota((LANES, width), 0) == (row & (LANES - 1)))
        all_tiles = dot(stack[...], jnp.concatenate([chosen, chosen], axis=0))
        for k in range(per_tile):
            here = jnp.broadcast_to(pos[k:k + 1, :], (8, LANES))
            low = here & (LANES - 1)
            masks = [(here >> 7) == i for i in range(src_tiles)]
            for at in range(by_dot, levels, 8):
                got = pick(coef_v[at:at + 8, 0:LANES], low)
                for i in range(1, src_tiles):
                    other = pick(coef_v[at:at + 8, i * LANES:(i + 1) * LANES], low)
                    got = jnp.where(masks[i], other, got)
                into[at:at + 8, k * LANES:(k + 1) * LANES] = got
            for at in range(0, by_dot, 8):
                lanes = slice(k * LANES, (k + 1) * LANES)
                got = all_tiles[at:at + 8, lanes]
                for i in range(1, src_tiles):
                    other = all_tiles[i * by_dot + at:i * by_dot + at + 8, lanes]
                    got = jnp.where(masks[i], other, got)
                into[at:at + 8, lanes] = got

    def serve(k, carry):
        peer = lax.rem(dev + far(k), n_dev)
        pos_copy(peer, peer).wait_recv()
        wanted(pos_in[peer], blk_out.at[peer])
        blk_copy(peer, dev).start()
        return carry

    lax.fori_loop(0, n_dev - 1, serve, 0)
    wanted(send_pos[pl.ds(pl.multiple_of(dev * 8, 8), 8), :], blk_in.at[dev])

    for load in loads[4:]:
        load.wait()
    for s in range(4):
        nbr = nbr_v[s:s + 1, :]
        edge_w[:, s * LANES:(s + 1) * LANES] = one_hot(iota((5 * LANES, LANES), 0) == nbr)

    def gather_own(table):
        hi, lo = table
        weights = edge_w[0:4 * LANES, :]
        across_v[...] = dot(hi, weights) + dot(lo, weights)

    def gather_far(turn):
        for copy in edge_copies(turn):
            copy.wait_recv()
        hi, lo = halves(edge_in[turn].T[:4 * levels])
        weights = edge_w[4 * LANES:5 * LANES, :]
        across_v[...] += dot(hi, weights) + dot(lo, weights)

    def operator(ref, emit):
        scale = met_v[...]
        flips = [flip_v[s:s + 1, :] == 1 for s in range(4)]

        def chunk(i, carry):
            at = pl.multiple_of(i * 8, 8)
            u = [ref[p, pl.ds(at, 8), :] for p in range(points)]
            acc = [None] * points
            touch = [0] * points
            for s in range(4):
                for t in range(4):
                    p = EDGE_POINT[s][t]
                    lanes = slice(s * LANES, (s + 1) * LANES)
                    same = across_v[pl.ds(pl.multiple_of(t * levels + at, 8), 8), lanes]
                    back = across_v[pl.ds(pl.multiple_of((3 - t) * levels + at, 8), 8), lanes]
                    value = jnp.where(flips[s], back, same)
                    acc[p] = value if acc[p] is None else acc[p] + value
                    touch[p] += 1
            for p in range(points):
                total = None if acc[p] is None else PENALTY * acc[p]
                for q in range(points):
                    weight = lap[p, q] - (PENALTY * touch[p] if p == q else 0.0)
                    if weight != 0.0:
                        term = np.float32(weight) * u[q]
                        total = term if total is None else total + term
                emit(i, at, p, scale * total)
            return carry

        lax.fori_loop(0, levels // 8, chunk, 0)

    gather_own(table)
    gather_far(0)

    def keep_first(i, at, p, value):
        first[p, pl.ds(at, 8), :] = value

    operator(field, keep_first)
    def arrived(k):
        peer = lax.rem(dev + n_dev - far(k), n_dev)
        blk_copy(peer, peer).wait_recv()
        return peer

    def place_blocks(peers, begin, last):
        for p in range(points):
            low = jnp.broadcast_to(lane[p:p + 1, :], (8, LANES))
            which = jnp.broadcast_to(tile[p:p + 1, :], (8, LANES))
            pairs = [(peer, k, which == peer * per_tile + k) for peer in peers for k in range(per_tile)]
            lanes = slice(p * LANES, (p + 1) * LANES)
            for at in range(0, levels, 8):
                value = None if begin else col_c[at:at + 8, lanes]
                for peer, k, mask in pairs:
                    other = pick(blk_in[peer, at:at + 8, k * LANES:(k + 1) * LANES], low)
                    value = other if value is None else jnp.where(mask, other, value)
                if last:
                    lev_c[pl.ds(at * points + p, 8, stride=points), :] = value
                else:
                    col_c[at:at + 8, lanes] = value

    table = table_of(first)
    send_edges(table, 1)
    gather_own(table)
    place_blocks([dev] + [arrived(k) for k in range(n_dev - 5)], True, False)
    gather_far(1)

    def keep_stepped(i, at, p, value):
        lev_b[pl.ds(i * (8 * points) + p, 8, stride=points), :] = (
            field[p, pl.ds(at, 8), :] - HYPER * value
        )

    operator(first, keep_stepped)
    place_blocks([arrived(k) for k in range(n_dev - 5, n_dev - 3)], False, False)
    place_blocks([arrived(k) for k in range(n_dev - 3, n_dev - 1)], False, True)

    def finish(d, carry):
        peer = lax.rem(dev + d, n_dev)
        pos_copy(peer, dev).wait_send()
        blk_copy(peer, dev).wait_send()
        return carry

    lax.fori_loop(1, n_dev, finish, 0)
    for turn in range(2):
        for copy in edge_copies(turn):
            copy.wait_send()


def solve_kernel(levels, lev_c, lev_b, out, out_v, lev_u, lev_y, sem):
    points = 16

    def level(ref, k):
        return ref[pl.ds(pl.multiple_of(k * points, points), points), :]

    def put(ref, k, value):
        ref[pl.ds(pl.multiple_of(k * points, points), points), :] = value

    mid = levels // 2
    zero = jnp.zeros((points, LANES), F32)
    c_first = level(lev_c, 0)
    batch = 4

    def eliminate(step, carry):
        e, c_up, y, er, u, g, c_dn, z, gr, v = carry
        for part in range(batch):
            k = step * batch + part
            c1 = level(lev_c, k + 1)
            r = pl.reciprocal(e + c1)
            u = c1 * r
            y = (level(lev_b, k) + c_up * y) * r
            er = e * r
            e = 1.0 + c1 * er
            c_up = c1
            put(lev_u, k, u)
            put(lev_y, k, y)
            m = levels - 1 - k
            cm = level(lev_c, m)
            r = pl.reciprocal(g + cm)
            v = cm * r
            z = (level(lev_b, m) + c_dn * z) * r
            gr = g * r
            g = 1.0 + cm * gr
            c_dn = cm
            put(lev_u, m, v)
            put(lev_y, m, z)
        return e, c_up, y, er, u, g, c_dn, z, gr, v

    start = (1.0 + c_first, c_first, zero, zero, zero, zero + 1.0, zero, zero, zero, zero)
    e, c_up, y, er, u, g, c_dn, z, gr, v = lax.fori_loop(0, mid // batch, eliminate, start)
    x_top = (y + u * z) / (er + u * gr)
    x_bot = z + v * x_top
    put(out_v, mid - 1, x_top)
    put(out_v, mid, x_bot)

    def substitute(k, carry):
        x_up, x_dn = carry
        i = mid - 1 - k
        m = mid + k
        x_up = level(lev_y, i) + level(lev_u, i) * x_up
        x_dn = level(lev_y, m) + level(lev_u, m) * x_dn
        put(out_v, i, x_up)
        put(out_v, m, x_dn)
        return x_up, x_dn

    copies = []

    def write(low, high):
        rows = pl.ds(low * points, (high - low) * points)
        copy = pltpu.make_async_copy(out_v.at[rows, :], out.at[rows, :], sem.at[len(copies)])
        copy.start()
        copies.append(copy)

    carry = (x_top, x_bot)
    done = 0
    for k in range(1, mid):
        carry = substitute(k, carry)
        if k % 6 == 5 or k == mid - 1:
            write(mid - 1 - k, mid - done)
            write(mid + done, mid + k + 1)
            done = k + 1
    for copy in copies:
        copy.wait()


def on_device(n_grp, n_dev, tracer, metric, coef, nbr_slot, edge_flip, send_slot, span_slot):
    levels, points, elems = tracer.shape
    cols = coef.shape[1]
    width = max(cols // n_dev, LANES)
    rows = levels * points
    vmem = pltpu.VMEM
    dma = pltpu.SemaphoreType.DMA
    hbm_spec = pl.BlockSpec(memory_space=pltpu.HBM)
    vmem_spec = pl.BlockSpec(memory_space=vmem)
    flat = jax.ShapeDtypeStruct((rows, elems), F32)
    mixing, stepped = pl.pallas_call(
        functools.partial(kernel, n_grp, n_dev, levels, cols),
        out_shape=[flat, flat],
        in_specs=[hbm_spec] * 7,
        out_specs=[vmem_spec, vmem_spec],
        scratch_shapes=[
            vmem((rows, elems), F32),
            vmem((1, elems), F32),
            vmem((levels, cols), F32),
            vmem((4, elems), I32),
            vmem((4, elems), I32),
            vmem((1, 48), I32),
            vmem((points, elems), I32),
            vmem((n_dev * 8, LANES), F32),
            vmem((n_dev, 8, LANES), F32),
            vmem((cols // LANES * (levels // 2 // 16 * 16), 2 * LANES), BF16),
            vmem((n_dev, levels, width), F32),
            vmem((n_dev, levels, width), F32),
            vmem((LANES, cols), BF16),
            vmem((5 * LANES, 4 * LANES), BF16),
            vmem((4 * LANES, LANES), BF16),
            vmem((2, LANES, 3 * LANES), F32),
            vmem((2, LANES, 3 * LANES), F32),
            vmem((4 * levels, 4 * LANES), F32),
            vmem((points, levels, elems), F32),
            vmem((points, levels, elems), F32),
            vmem((levels, cols), F32),
            dma((7,)),
            dma((n_dev,)),
            dma((n_dev,)),
            dma((n_dev,)),
            dma((n_dev,)),
            dma((2, 4)),
            dma((2, 4)),
        ],
        compiler_params=pltpu.CompilerParams(
            collective_id=0, has_side_effects=True, vmem_limit_bytes=40 * 2**20
        ),
        cost_estimate=pl.CostEstimate(flops=10**9, bytes_accessed=4 * 10**6, transcendentals=0),
        name="hyper_mix",
    )(
        *[
            pltpu.with_memory_space_constraint(array, pltpu.HBM)
            for array in (
                tracer.reshape(rows, elems),
                metric.reshape(1, elems),
                coef,
                nbr_slot,
                edge_flip,
                send_slot.reshape(1, 48),
                span_slot,
            )
        ]
    )
    mixed = pl.pallas_call(
        functools.partial(solve_kernel, levels),
        out_shape=flat,
        in_specs=[vmem_spec, vmem_spec],
        out_specs=hbm_spec,
        scratch_shapes=[vmem((rows, elems), F32)] * 3 + [dma((2 * (levels // 12 + 1),))],
        compiler_params=pltpu.CompilerParams(vmem_limit_bytes=40 * 2**20),
        cost_estimate=pl.CostEstimate(flops=10**7, bytes_accessed=2 * 10**6, transcendentals=0),
        name="column_solve",
    )(mixing, stepped)
    return mixed.reshape(tracer.shape)


def solution(mesh):
    in_specs = (
        P(None, None, ("grp", "dev")),
        P(("grp", "dev")),
        P(None, ("grp", "dev")),
        P(None, ("grp", "dev")),
        P(None, ("grp", "dev")),
        P(("grp", "dev")),
        P(None, ("grp", "dev")),
    )
    out_specs = P(None, None, ("grp", "dev"))
    body = functools.partial(on_device, mesh.shape["grp"], mesh.shape["dev"])
    return jax.shard_map(body, mesh=mesh, in_specs=in_specs, out_specs=out_specs, check_vma=False)
```

```python
import functools

import jax
import jax.numpy as jnp
import numpy as np
from jax import lax
from jax.experimental import pallas as pl
from jax.experimental.pallas import tpu as pltpu
from jax.sharding import PartitionSpec as P

PENALTY = 10.0
HYPER = 0.0001
LANES = 128
MESH = pl.DeviceIdType.MESH
F32 = jnp.float32
BF16 = jnp.bfloat16
I32 = jnp.int32

EDGE_POINT = [[0, 1, 2, 3], [3, 7, 11, 15], [12, 13, 14, 15], [0, 4, 8, 12]]
EDGE_ROWS = [(0, 16, 1, 0), (16, 16, -1, 0), (32, 8, 0, 1), (40, 8, 0, -1)]


def gll_laplacian():
    gll_nodes = np.array([-1.0, -1.0 / np.sqrt(5.0), 1.0 / np.sqrt(5.0), 1.0])
    weights = np.array([1.0 / 6.0, 5.0 / 6.0, 5.0 / 6.0, 1.0 / 6.0])
    lambdas = np.ones(4)
    for jdx in range(4):
        for kdx in range(4):
            if kdx != jdx:
                lambdas[jdx] = lambdas[jdx] / (gll_nodes[jdx] - gll_nodes[kdx])
    derivative = np.zeros((4, 4))
    for idx in range(4):
        for jdx in range(4):
            if idx != jdx:
                derivative[idx, jdx] = (
                    lambdas[jdx] / lambdas[idx] / (gll_nodes[idx] - gll_nodes[jdx])
                )
        derivative[idx, idx] = -np.sum(derivative[idx])
    stiffness = -(derivative.T * weights[None, :] @ derivative) / weights[:, None]
    identity = np.eye(4)
    return np.kron(stiffness, identity) + np.kron(identity, stiffness)


def iota(shape, dim):
    return lax.broadcasted_iota(I32, shape, dim)


def one_hot(cond):
    return jnp.where(cond, 1.0, 0.0).astype(BF16)


def halves(value):
    hi = value.astype(BF16)
    lo = (value - hi.astype(F32)).astype(BF16)
    return hi, lo


def pick(value, lanes):
    return jnp.take_along_axis(value, lanes, axis=1, mode="promise_in_bounds")


def dot(a, b):
    return jnp.dot(a, b, preferred_element_type=F32)


def kernel(
    n_grp, n_dev, levels, cols,
    tr_h, met_h, coef_h, nbr_h, flip_h, send_h, span_h,
    lev_c, lev_b,
    tr_v, met_v, coef_v, nbr_v, flip_v, send_v, span_v,
    send_pos, pos_in, stack, blk_out, blk_in, spread_w,
    edge_w, send_w, edge_out, edge_in, across_v,
    field, first, col_c,
    load_sem, pos_ssem, pos_rsem, blk_ssem, blk_rsem, edge_ssem, edge_rsem,
):
    grp, dev = lax.axis_index("grp"), lax.axis_index("dev")
    points = 16
    per_peer = cols // n_dev
    width = max(per_peer, LANES)
    per_tile = width // LANES
    src_tiles = cols // LANES
    lap = gll_laplacian()

    loads = [
        pltpu.make_async_copy(src, dst, load_sem.at[i])
        for i, (src, dst) in enumerate(
            [(span_h, span_v), (tr_h, tr_v), (send_h, send_v), (coef_h, coef_v),
             (nbr_h, nbr_v), (flip_h, flip_v), (met_h, met_v)]
        )
    ]
    for load in loads:
        load.start()

    barrier = pltpu.get_barrier_semaphore()
    for d in range(1, n_dev):
        pl.semaphore_signal(
            barrier, inc=1, device_id=(grp, lax.rem(dev + d, n_dev)), device_id_type=MESH
        )
    for step in (1, n_grp - 1):
        pl.semaphore_signal(
            barrier, inc=1, device_id=(lax.rem(grp + step, n_grp), dev), device_id_type=MESH
        )

    loads[0].wait()
    span = span_v[...]
    shift = cols.bit_length() - 1
    target = span >> shift
    place = span & (cols - 1)
    hits = jnp.concatenate(
        [jnp.where(target == r, 1.0, 0.0) for r in range(n_dev)], axis=0
    ).astype(BF16)
    count = n_dev * points
    before = one_hot(iota((LANES, LANES), 0) < iota((LANES, LANES), 1))
    along = dot(hits, before)
    totals = dot(hits, jnp.ones((LANES, LANES), BF16))
    row_i, col_i = iota((count, count), 0), iota((count, count), 1)
    earlier = one_hot((col_i < row_i) & ((col_i >> 4) == (row_i >> 4)))
    ranks = along + dot(earlier, totals.astype(BF16))
    rank = jnp.zeros((points, LANES), F32)
    for r in range(n_dev):
        rank = jnp.where(target == r, ranks[r * points:(r + 1) * points], rank)
    rank = rank.astype(I32)
    sub = rank >> 7
    lane = rank & (LANES - 1)
    tile = target * per_tile + sub
    row8 = target * 8 + sub
    place_hi = (place >> 7).astype(F32)
    place_lo = (place & (LANES - 1)).astype(F32)
    rows_out = n_dev * 8
    lists = []
    for p in range(points):
        spread_w[0:LANES, p * LANES:(p + 1) * LANES] = one_hot(
            iota((LANES, LANES), 0) == lane[p:p + 1, :]
        )
        mine = iota((rows_out, LANES), 0) == row8[p:p + 1, :]
        lists.append(
            jnp.concatenate(
                [jnp.where(mine, place_hi[p:p + 1, :], 0.0), jnp.where(mine, place_lo[p:p + 1, :], 0.0)],
                axis=0,
            ).astype(BF16)
        )
    packed = lax.dot_general(
        jnp.concatenate(lists, axis=1),
        spread_w[0:LANES, :],
        (((1,), (1,)), ((), ())),
        preferred_element_type=F32,
    )
    send_pos[...] = packed[:rows_out] * 128.0 + packed[rows_out:]
    edge_in[0, 48:LANES, :] = jnp.zeros((LANES - 48, 3 * LANES), F32)
    edge_in[1, 48:LANES, :] = jnp.zeros((LANES - 48, 3 * LANES), F32)
    send_w[...] = jnp.zeros(send_w.shape, BF16)

    pl.semaphore_wait(barrier, n_dev + 1)

    def pos_copy(peer, slot):
        return pltpu.make_async_remote_copy(
            src_ref=send_pos.at[pl.ds(pl.multiple_of(peer * 8, 8), 8), :],
            dst_ref=pos_in.at[slot],
            send_sem=pos_ssem.at[peer],
            recv_sem=pos_rsem.at[slot],
            device_id=(grp, peer),
            device_id_type=MESH,
        )

    def blk_copy(peer, slot):
        return pltpu.make_async_remote_copy(
            src_ref=blk_out.at[peer],
            dst_ref=blk_in.at[slot],
            send_sem=blk_ssem.at[peer],
            recv_sem=blk_rsem.at[slot],
            device_id=(grp, peer),
            device_id_type=MESH,
        )

    def edge_copies(turn):
        return [
            pltpu.make_async_remote_copy(
                src_ref=edge_out.at[turn, pl.ds(at, rows), :],
                dst_ref=edge_in.at[turn, pl.ds(at, rows), :],
                send_sem=edge_ssem.at[turn, k],
                recv_sem=edge_rsem.at[turn, k],
                device_id=(lax.rem(grp + n_grp + dg, n_grp), lax.rem(dev + n_dev + dv, n_dev)),
                device_id_type=MESH,
            )
            for k, (at, rows, dg, dv) in enumerate(EDGE_ROWS)
        ]

    def far(k):
        return n_dev // 2 + (1 - 2 * (k % 2)) * ((k + 1) // 2)

    def start_pos(k, carry):
        pos_copy(lax.rem(dev + n_dev - far(k), n_dev), dev).start()
        return carry

    lax.fori_loop(0, n_dev - 1, start_pos, 0)

    loads[1].wait()
    loads[2].wait()
    send_w[:, 0:48] = one_hot(iota((4 * LANES, 48), 0) == send_v[...])
    for p in range(points):
        field[p] = tr_v[pl.ds(p, levels, stride=points), :]

    def table_of(ref):
        return halves(
            jnp.concatenate(
                [
                    jnp.concatenate([ref[EDGE_POINT[s][t]] for s in range(4)], axis=1)
                    for t in range(4)
                ],
                axis=0,
            )
        )

    def send_edges(table, turn):
        hi, lo = table
        sent = dot(hi, send_w[...]) + dot(lo, send_w[...])
        rest = jnp.zeros((3 * LANES - 4 * levels, LANES), F32)
        edge_out[turn] = jnp.concatenate([sent, rest], axis=0).T
        for copy in edge_copies(turn):
            copy.start()

    table = table_of(field)
    send_edges(table, 0)

    loads[3].wait()

    by_dot = levels // 2 // 16 * 16
    coef_hi, coef_lo = halves(
        jnp.concatenate(
            [coef_v[0:by_dot, i * LANES:(i + 1) * LANES] for i in range(src_tiles)], axis=0
        )
    )
    stack[:, 0:LANES] = coef_hi
    stack[:, LANES:2 * LANES] = coef_lo

    def wanted(pos_tile, into):
        pos = pos_tile.astype(I32)
        row = jnp.concatenate([pos[k:k + 1, :] for k in range(per_tile)], axis=1)
        chosen = one_hot(iota((LANES, width), 0) == (row & (LANES - 1)))
        all_tiles = dot(stack[...], jnp.concatenate([chosen, chosen], axis=0))
        for k in range(per_tile):
            here = jnp.broadcast_to(pos[k:k + 1, :], (8, LANES))
            low = here & (LANES - 1)
            masks = [(here >> 7) == i for i in range(src_tiles)]
            for at in range(by_dot, levels, 8):
                got = pick(coef_v[at:at + 8, 0:LANES], low)
                for i in range(1, src_tiles):
                    other = pick(coef_v[at:at + 8, i * LANES:(i + 1) * LANES], low)
                    got = jnp.where(masks[i], other, got)
                into[at:at + 8, k * LANES:(k + 1) * LANES] = got
            for at in range(0, by_dot, 8):
                lanes = slice(k * LANES, (k + 1) * LANES)
                got = all_tiles[at:at + 8, lanes]
                for i in range(1, src_tiles):
                    other = all_tiles[i * by_dot + at:i * by_dot + at + 8, lanes]
                    got = jnp.where(masks[i], other, got)
                into[at:at + 8, lanes] = got

    def serve(k, carry):
        peer = lax.rem(dev + far(k), n_dev)
        pos_copy(peer, peer).wait_recv()
        wanted(pos_in[peer], blk_out.at[peer])
        blk_copy(peer, dev).start()
        return carry

    lax.fori_loop(0, n_dev - 1, serve, 0)
    wanted(send_pos[pl.ds(pl.multiple_of(dev * 8, 8), 8), :], blk_in.at[dev])

    for load in loads[4:]:
        load.wait()
    for s in range(4):
        nbr = nbr_v[s:s + 1, :]
        edge_w[:, s * LANES:(s + 1) * LANES] = one_hot(iota((5 * LANES, LANES), 0) == nbr)

    def gather_own(table):
        hi, lo = table
        weights = edge_w[0:4 * LANES, :]
        across_v[...] = dot(hi, weights) + dot(lo, weights)

    def gather_far(turn):
        for copy in edge_copies(turn):
            copy.wait_recv()
        hi, lo = halves(edge_in[turn].T[:4 * levels])
        weights = edge_w[4 * LANES:5 * LANES, :]
        across_v[...] += dot(hi, weights) + dot(lo, weights)

    def operator(ref, emit):
        scale = met_v[...]
        flips = [flip_v[s:s + 1, :] == 1 for s in range(4)]

        def chunk(i, carry):
            at = pl.multiple_of(i * 8, 8)
            u = [ref[p, pl.ds(at, 8), :] for p in range(points)]
            acc = [None] * points
            touch = [0] * points
            for s in range(4):
                for t in range(4):
                    p = EDGE_POINT[s][t]
                    lanes = slice(s * LANES, (s + 1) * LANES)
                    same = across_v[pl.ds(pl.multiple_of(t * levels + at, 8), 8), lanes]
                    back = across_v[pl.ds(pl.multiple_of((3 - t) * levels + at, 8), 8), lanes]
                    value = jnp.where(flips[s], back, same)
                    acc[p] = value if acc[p] is None else acc[p] + value
                    touch[p] += 1
            for p in range(points):
                total = None if acc[p] is None else PENALTY * acc[p]
                for q in range(points):
                    weight = lap[p, q] - (PENALTY * touch[p] if p == q else 0.0)
                    if weight != 0.0:
                        term = np.float32(weight) * u[q]
                        total = term if total is None else total + term
                emit(i, at, p, scale * total)
            return carry

        lax.fori_loop(0, levels // 8, chunk, 0)

    gather_own(table)
    gather_far(0)

    def keep_first(i, at, p, value):
        first[p, pl.ds(at, 8), :] = value

    operator(field, keep_first)
    def arrived(k):
        peer = lax.rem(dev + n_dev - far(k), n_dev)
        blk_copy(peer, peer).wait_recv()
        return peer

    def place_blocks(peers, begin, last):
        for p in range(points):
            low = jnp.broadcast_to(lane[p:p + 1, :], (8, LANES))
            which = jnp.broadcast_to(tile[p:p + 1, :], (8, LANES))
            pairs = [(peer, k, which == peer * per_tile + k) for peer in peers for k in range(per_tile)]
            lanes = slice(p * LANES, (p + 1) * LANES)
            for at in range(0, levels, 8):
                value = None if begin else col_c[at:at + 8, lanes]
                for peer, k, mask in pairs:
                    other = pick(blk_in[peer, at:at + 8, k * LANES:(k + 1) * LANES], low)
                    value = other if value is None else jnp.where(mask, other, value)
                if last:
                    lev_c[pl.ds(at * points + p, 8, stride=points), :] = value
                else:
                    col_c[at:at + 8, lanes] = value

    table = table_of(first)
    send_edges(table, 1)
    gather_own(table)
    place_blocks([dev] + [arrived(k) for k in range(n_dev - 7)], True, False)
    gather_far(1)

    def keep_stepped(i, at, p, value):
        lev_b[pl.ds(i * (8 * points) + p, 8, stride=points), :] = (
            field[p, pl.ds(at, 8), :] - HYPER * value
        )

    operator(first, keep_stepped)
    place_blocks([arrived(k) for k in range(n_dev - 7, n_dev - 3)], False, False)
    place_blocks([arrived(k) for k in range(n_dev - 3, n_dev - 1)], False, True)

    def finish(d, carry):
        peer = lax.rem(dev + d, n_dev)
        pos_copy(peer, dev).wait_send()
        blk_copy(peer, dev).wait_send()
        return carry

    lax.fori_loop(1, n_dev, finish, 0)
    for turn in range(2):
        for copy in edge_copies(turn):
            copy.wait_send()


def solve_kernel(levels, lev_c, lev_b, out, out_v, lev_u, lev_y, sem):
    points = 16

    def level(ref, k):
        return ref[pl.ds(pl.multiple_of(k * points, points), points), :]

    def put(ref, k, value):
        ref[pl.ds(pl.multiple_of(k * points, points), points), :] = value

    mid = levels // 2
    zero = jnp.zeros((points, LANES), F32)
    c_first = level(lev_c, 0)
    batch = 4

    def eliminate(step, carry):
        e, c_up, y, er, u, g, c_dn, z, gr, v = carry
        for part in range(batch):
            k = step * batch + part
            c1 = level(lev_c, k + 1)
            r = pl.reciprocal(e + c1)
            u = c1 * r
            y = (level(lev_b, k) + c_up * y) * r
            er = e * r
            e = 1.0 + c1 * er
            c_up = c1
            put(lev_u, k, u)
            put(lev_y, k, y)
            m = levels - 1 - k
            cm = level(lev_c, m)
            r = pl.reciprocal(g + cm)
            v = cm * r
            z = (level(lev_b, m) + c_dn * z) * r
            gr = g * r
            g = 1.0 + cm * gr
            c_dn = cm
            put(lev_u, m, v)
            put(lev_y, m, z)
        return e, c_up, y, er, u, g, c_dn, z, gr, v

    start = (1.0 + c_first, c_first, zero, zero, zero, zero + 1.0, zero, zero, zero, zero)
    e, c_up, y, er, u, g, c_dn, z, gr, v = lax.fori_loop(0, mid // batch, eliminate, start)
    x_top = (y + u * z) / (er + u * gr)
    x_bot = z + v * x_top
    put(out_v, mid - 1, x_top)
    put(out_v, mid, x_bot)

    def substitute(k, carry):
        x_up, x_dn = carry
        i = mid - 1 - k
        m = mid + k
        x_up = level(lev_y, i) + level(lev_u, i) * x_up
        x_dn = level(lev_y, m) + level(lev_u, m) * x_dn
        put(out_v, i, x_up)
        put(out_v, m, x_dn)
        return x_up, x_dn

    copies = []

    def write(low, high):
        rows = pl.ds(low * points, (high - low) * points)
        copy = pltpu.make_async_copy(out_v.at[rows, :], out.at[rows, :], sem.at[len(copies)])
        copy.start()
        copies.append(copy)

    carry = (x_top, x_bot)
    done = 0
    for k in range(1, mid):
        carry = substitute(k, carry)
        if k % 6 == 5 or k == mid - 1:
            write(mid - 1 - k, mid - done)
            write(mid + done, mid + k + 1)
            done = k + 1
    for copy in copies:
        copy.wait()


def on_device(n_grp, n_dev, tracer, metric, coef, nbr_slot, edge_flip, send_slot, span_slot):
    levels, points, elems = tracer.shape
    cols = coef.shape[1]
    width = max(cols // n_dev, LANES)
    rows = levels * points
    vmem = pltpu.VMEM
    dma = pltpu.SemaphoreType.DMA
    hbm_spec = pl.BlockSpec(memory_space=pltpu.HBM)
    vmem_spec = pl.BlockSpec(memory_space=vmem)
    flat = jax.ShapeDtypeStruct((rows, elems), F32)
    mixing, stepped = pl.pallas_call(
        functools.partial(kernel, n_grp, n_dev, levels, cols),
        out_shape=[flat, flat],
        in_specs=[hbm_spec] * 7,
        out_specs=[vmem_spec, vmem_spec],
        scratch_shapes=[
            vmem((rows, elems), F32),
            vmem((1, elems), F32),
            vmem((levels, cols), F32),
            vmem((4, elems), I32),
            vmem((4, elems), I32),
            vmem((1, 48), I32),
            vmem((points, elems), I32),
            vmem((n_dev * 8, LANES), F32),
            vmem((n_dev, 8, LANES), F32),
            vmem((cols // LANES * (levels // 2 // 16 * 16), 2 * LANES), BF16),
            vmem((n_dev, levels, width), F32),
            vmem((n_dev, levels, width), F32),
            vmem((LANES, cols), BF16),
            vmem((5 * LANES, 4 * LANES), BF16),
            vmem((4 * LANES, LANES), BF16),
            vmem((2, LANES, 3 * LANES), F32),
            vmem((2, LANES, 3 * LANES), F32),
            vmem((4 * levels, 4 * LANES), F32),
            vmem((points, levels, elems), F32),
            vmem((points, levels, elems), F32),
            vmem((levels, cols), F32),
            dma((7,)),
            dma((n_dev,)),
            dma((n_dev,)),
            dma((n_dev,)),
            dma((n_dev,)),
            dma((2, 4)),
            dma((2, 4)),
        ],
        compiler_params=pltpu.CompilerParams(
            collective_id=0, has_side_effects=True, vmem_limit_bytes=40 * 2**20
        ),
        cost_estimate=pl.CostEstimate(flops=10**9, bytes_accessed=4 * 10**6, transcendentals=0),
        name="hyper_mix",
    )(
        *[
            pltpu.with_memory_space_constraint(array, pltpu.HBM)
            for array in (
                tracer.reshape(rows, elems),
                metric.reshape(1, elems),
                coef,
                nbr_slot,
                edge_flip,
                send_slot.reshape(1, 48),
                span_slot,
            )
        ]
    )
    mixed = pl.pallas_call(
        functools.partial(solve_kernel, levels),
        out_shape=flat,
        in_specs=[vmem_spec, vmem_spec],
        out_specs=hbm_spec,
        scratch_shapes=[vmem((rows, elems), F32)] * 3 + [dma((2 * (levels // 12 + 1),))],
        compiler_params=pltpu.CompilerParams(vmem_limit_bytes=40 * 2**20),
        cost_estimate=pl.CostEstimate(flops=10**7, bytes_accessed=2 * 10**6, transcendentals=0),
        name="column_solve",
    )(mixing, stepped)
    return mixed.reshape(tracer.shape)


def solution(mesh):
    in_specs = (
        P(None, None, ("grp", "dev")),
        P(("grp", "dev")),
        P(None, ("grp", "dev")),
        P(None, ("grp", "dev")),
        P(None, ("grp", "dev")),
        P(("grp", "dev")),
        P(None, ("grp", "dev")),
    )
    out_specs = P(None, None, ("grp", "dev"))
    body = functools.partial(on_device, mesh.shape["grp"], mesh.shape["dev"])
    return jax.shard_map(body, mesh=mesh, in_specs=in_specs, out_specs=out_specs, check_vma=False)
```
